256 devices in a mesh: role: 2 (over core), gx: 16 (over z, y_hi), gy: 8 (over x, y_lo).
Axes of the slice: x: 4, y: 4 (y_hi: 2, y_lo: 2; y = y_hi * 2 + y_lo), z: 8, core: 2. Of those that a mesh axis runs over, the one named last changes fastest.
Arguments:
- velocity: float32 [3, 384, 384, 128], P(None, 'gx', ('role', 'gy')), may hold values from -5 to 5
- target_field: float32 [3, 384, 384, 128], P(None, 'gx', ('role', 'gy')), may hold values from -4 to 4
- w_in: bfloat16 [1536, 512], replicated, may hold values from -0.15625 to 0.15625
- w_mid: bfloat16 [512, 512], replicated, may hold values from -0.25 to 0.25
- w_out: bfloat16 [512, 1536], replicated, may hold values from -0.25 to 0.25
- moment_one: float32 [1835008], P(('role', 'gx', 'gy')), may hold values from -5 to 5
- moment_two: float32 [1835008], P(('role', 'gx', 'gy')), may hold values from 0.01 to 0.1
- picks: int32 [8192], P(('role', 'gx', 'gy')), may hold values from 0 to 59
- owners: int32 [8192], P(('role', 'gx', 'gy')), may hold values from 0 to 15
- counts: int32 [16, 16], P(('role', 'gy'), 'gx'), may hold values from 1 to 32, 256 in all within a row
Outputs:
- velocity_next: float32 [3, 384, 384, 128], P(None, 'gx', ('role', 'gy'))
- direction: float32 [1835008], P(('role', 'gx', 'gy'))
The draws below stay inside these ranges and needn't reach their ends.
Inputs may be any that keep to these rules, and one draw needn't show every extreme that they name: Each row of counts sums to 256 and its largest entry is 32.
All inputs are finite; a program needn't handle non-finite values. No bound on the sum of `counts` on one device may be relied on, other than what follows from the above.
Results may differ from the reference program's by a relative error of at most 0.0085.
The reference program's roundings to bfloat16 on the way count: a program that leaves them out, or rounds other values in their place, can miss the bound.
Values sent between devices are 32-bit elements; how exact they have to be, the bound alone decides.
A program may use at most 192 MiB of HBM per device.

```python
import math
import jax
import jax.numpy as jnp
import numpy as np

BLOCK = 8
HID = 512
CX = 24
CY = 24
NZ = 128
PICK_MEAN = 16
ADAM_STEP = 10
PICK_MAX = 32
CLOSE = 1536
NX = 384
NY = 384
ANCHORS = 60
PARAMS = 1835008
N_ROLE = 2
N_GX = 16
N_GY = 8
DEVICES = 256


def touch_ends(drawn, key, smallest, top_value):
    spot = [jax.random.randint(jax.random.fold_in(key, axis), (), 0, length) for axis, length in enumerate(drawn.shape)]
    widest = drawn.shape.index(max(drawn.shape))
    next_to = spot[:widest] + [(spot[widest] + 1) % drawn.shape[widest]] + spot[widest + 1:]
    return drawn.at[tuple(spot)].set(smallest).at[tuple(next_to)].set(top_value)


def steps_of(own_key, shape, shards, smallest, largest):
    level, own = 1.0, jax.random.fold_in(own_key, 6)
    for axis_at, shards_of in shards:
        draws = jnp.exp(jax.random.uniform(jax.random.fold_in(own, axis_at), (shards_of,), jnp.float32, smallest / len(shards), largest / len(shards)))
        level = level * jnp.repeat(draws, shape[axis_at] // shards_of).reshape([-1 if axis == axis_at else 1 for axis in range(len(shape))])
    return level


def rank_bounds(count, lean):
    portions = [(1 << 20) // math.isqrt(rank ** lean) + 1 for rank in range(1, count + 1)]
    deviation = 1 + sum(portions) // (1 << 30)
    return np.cumsum(np.array([max(1, weight // deviation) for weight in portions]))


def skewed_ids(own_key, shape, count, slope):
    table = rank_bounds(count, slope)
    ticket = jax.random.randint(jax.random.fold_in(own_key, 1), shape, 0, int(table[count - 1]))
    standing = jnp.searchsorted(jnp.asarray(table, jnp.int32), ticket, side="right")
    return jax.random.permutation(jax.random.fold_in(own_key, 2), count)[standing].astype(jnp.int32)


def length_profile(amount, total, limit, skew):
    weights = [(1 << 20) // math.isqrt(rank ** skew) + 1 for rank in range(2, amount + 1)]
    rest, holding = total - limit - (amount - 1), [1] * (amount - 1)
    while rest > 0:
        free = [i for i in range(amount - 1) if holding[i] < limit]
        whole, left = sum([weights[i] for i in free]), rest
        for i in free:
            addition = min(limit - holding[i], max(1, left * weights[i] // whole), rest)
            holding[i] = holding[i] + addition
            rest = rest - addition
    return np.array([limit] + holding)


def uneven(rng, count, total, most, lean):
    if count == 2:
        one = jax.random.randint(rng, (), max(1, total - most), min(most, total - 1) + 1)
        return jnp.stack([one, total - one])
    sizes = jnp.asarray(length_profile(count, total, most, lean), jnp.int32)
    twos = (count - 1) // 2
    giver, taker = sizes[1:1 + 2 * twos:2], sizes[2:2 + 2 * twos:2]
    margin = jnp.minimum(giver - 1, most - taker)
    shifted = jax.random.randint(jax.random.fold_in(rng, 1), (twos,), 0, 1 << 20) % (margin + 1)
    sizes = sizes.at[1:1 + 2 * twos:2].set(giver - shifted).at[2:2 + 2 * twos:2].set(taker + shifted)
    return sizes[jax.random.permutation(jax.random.fold_in(rng, 2), count)]


def bell_draw(own_key, shape, width, reach, cuts=(), kind=jnp.bfloat16):
    result = jax.random.normal(own_key, shape, jnp.float32) * width
    if len(cuts) > 0:
        result = steps_of(own_key, shape, cuts, -0.22, 0.18) * result
    return jnp.clip(result, min=-reach, max=reach).astype(kind)


def setup_inputs(seed: int = 0) -> dict:
    key_list = jax.random.split(jax.random.key(seed), 11)
    velocity = bell_draw(key_list[0], (3, NX, NY, NZ), 1.0, 5.0, ((1, 16), (2, 16)), jnp.float32)
    target_field = bell_draw(key_list[1], (3, NX, NY, NZ), 0.5, 4.0, ((1, 16), (2, 16)), jnp.float32)
    w_in = bell_draw(key_list[2], (CLOSE, HID), CLOSE ** -0.5, 0.15625)
    w_mid = bell_draw(key_list[3], (HID, HID), HID ** -0.5, 0.25)
    w_out = bell_draw(key_list[4], (HID, CLOSE), HID ** -0.5, 0.25)
    moment_one = bell_draw(key_list[5], (PARAMS,), 1.0, 5.0, ((0, 256),), jnp.float32)
    moment_two = jnp.clip(jnp.exp(math.log(0.1) - 2.3025851 * jax.random.uniform(key_list[6], (PARAMS,), jnp.float32) ** steps_of(key_list[6], (PARAMS,), ((0, 256),), -0.2, 0.2)), 0.01, 0.1)
    picks = touch_ends(skewed_ids(key_list[7], (DEVICES * PICK_MAX,), ANCHORS, 2), jax.random.fold_in(key_list[7], 3), 0, ANCHORS - 1).astype(jnp.int32)
    owners = touch_ends(skewed_ids(key_list[8], (DEVICES * PICK_MAX,), N_GX, 2), jax.random.fold_in(key_list[8], 3), 0, N_GX - 1).astype(jnp.int32)
    counts = jax.vmap(lambda own: uneven(own, N_GX, PICK_MEAN * N_GX, PICK_MAX, 2))(jax.random.split(key_list[9], (N_ROLE * N_GY))).reshape((N_ROLE * N_GY, N_GX)).astype(jnp.int32)
    return {"velocity": velocity, "target_field": target_field, "w_in": w_in, "w_mid": w_mid, "w_out": w_out, "moment_one": moment_one, "moment_two": moment_two, "picks": picks, "owners": owners, "counts": counts}


TIME_STEP = 0.2
VISCOSITY = 0.05
BETA_ONE = 0.9
BETA_TWO = 0.999
EPSILON = 1e-08

def blocks_of(field):
    comp_count, size_first, size_second, size_third = field.shape
    pieces = field.reshape(comp_count, size_first // BLOCK, BLOCK, size_second // BLOCK, BLOCK, size_third // BLOCK, BLOCK)
    pieces = pieces.transpose(1, 3, 5, 0, 2, 4, 6)
    return pieces.reshape(-1, comp_count * BLOCK * BLOCK * BLOCK)

def field_of(block_rows, shape):
    comp_count, size_first, size_second, size_third = shape
    pieces = block_rows.reshape(size_first // BLOCK, size_second // BLOCK, size_third // BLOCK, comp_count, BLOCK, BLOCK, BLOCK)
    pieces = pieces.transpose(3, 0, 4, 1, 5, 2, 6)
    return pieces.reshape(comp_count, size_first, size_second, size_third)

def closure_rows(block_rows, w_in, w_mid, w_out):
    hidden_one = jax.nn.gelu(jnp.dot(block_rows, w_in, preferred_element_type=jnp.float32)).astype(jnp.bfloat16)
    hidden_two = jax.nn.gelu(jnp.dot(hidden_one, w_mid, preferred_element_type=jnp.float32)).astype(jnp.bfloat16)
    return jnp.dot(hidden_two, w_out, preferred_element_type=jnp.float32)

def tendency(field, block_rows, w_in, w_mid, w_out):
    closed = field_of(closure_rows(block_rows, w_in, w_mid, w_out), field.shape)
    components = []
    for component in range(3):
        values = field[component]
        first_up = jnp.roll(values, -1, 0)
        first_down = jnp.roll(values, 1, 0)
        second_up = jnp.roll(values, -1, 1)
        second_down = jnp.roll(values, 1, 1)
        third_up = jnp.roll(values, -1, 2)
        third_down = jnp.roll(values, 1, 2)
        advect = field[0] * ((first_up - first_down) * 0.5) + field[1] * ((second_up - second_down) * 0.5) + field[2] * ((third_up - third_down) * 0.5)
        spread = first_up + first_down + (second_up + second_down) + (third_up + third_down) - 6.0 * values
        components.append(VISCOSITY * spread - advect + closed[component])
    return jnp.stack(components)

def gelu_back(pre_act, upstream):
    unused_value, pull_back = jax.vjp(jax.nn.gelu, pre_act)
    return pull_back(upstream)[0]

def gradient(inputs, targets, row_weight, w_in, w_mid, w_out):
    pre_one = jnp.dot(inputs, w_in, preferred_element_type=jnp.float32)
    hidden_one = jax.nn.gelu(pre_one).astype(jnp.bfloat16)
    pre_two = jnp.dot(hidden_one, w_mid, preferred_element_type=jnp.float32)
    hidden_two = jax.nn.gelu(pre_two).astype(jnp.bfloat16)
    output = jnp.dot(hidden_two, w_out, preferred_element_type=jnp.float32)
    upstream = (2.0 * row_weight[:, None] * (output - targets.astype(jnp.float32))).astype(jnp.bfloat16)
    grad_out = jnp.dot(hidden_two.T, upstream, preferred_element_type=jnp.float32)
    back_two = gelu_back(pre_two, jnp.dot(upstream, w_out.T, preferred_element_type=jnp.float32)).astype(jnp.bfloat16)
    grad_mid = jnp.dot(hidden_one.T, back_two, preferred_element_type=jnp.float32)
    back_one = gelu_back(pre_one, jnp.dot(back_two, w_mid.T, preferred_element_type=jnp.float32)).astype(jnp.bfloat16)
    grad_in = jnp.dot(inputs.T, back_one, preferred_element_type=jnp.float32)
    return jnp.concatenate([grad_in.reshape(-1), grad_mid.reshape(-1), grad_out.reshape(-1)])

def adam_direction(moment_one, moment_two, grad_flat):
    moment_new = BETA_ONE * moment_one + (1.0 - BETA_ONE) * grad_flat
    second_new = BETA_TWO * moment_two + (1.0 - BETA_TWO) * grad_flat * grad_flat
    corrected = moment_new / (1.0 - BETA_ONE ** ADAM_STEP)
    return corrected / (jnp.sqrt(second_new / (1.0 - BETA_TWO ** ADAM_STEP)) + EPSILON)

def reference(velocity, target_field, w_in, w_mid, w_out, moment_one, moment_two, picks, owners, counts):
    first_rows = blocks_of(velocity).astype(jnp.bfloat16)
    section_one = velocity + TIME_STEP * tendency(velocity, first_rows, w_in, w_mid, w_out)
    second_rows = blocks_of(section_one).astype(jnp.bfloat16)
    velocity_next = 0.75 * velocity + 0.25 * (section_one + TIME_STEP * tendency(section_one, second_rows, w_in, w_mid, w_out))
    target_rows = blocks_of(target_field).astype(jnp.bfloat16)
    blocks_first = CX // BLOCK
    blocks_second = CY // BLOCK
    blocks_third = NZ // BLOCK
    mid_span = blocks_second - 1
    last_span = blocks_third - 1
    whole_second = NY // BLOCK
    flat_slot = jnp.arange(DEVICES * PICK_MAX, dtype=jnp.int32)
    device = flat_slot // PICK_MAX
    within = flat_slot % PICK_MAX
    role_index = device // (N_GX * N_GY)
    column = device // N_GY % N_GX
    group = role_index * N_GY + device % N_GY
    pick_count = counts[group, column]
    alive_mask = within < pick_count
    anchor_first = picks // (mid_span * last_span)
    anchor_second = picks // last_span % mid_span
    anchor_third = picks % last_span
    corner = jnp.arange(8, dtype=jnp.int32)
    block_index = ((column * blocks_first + anchor_first)[:, None] + corner // 4) * whole_second
    block_index = (block_index + (group * blocks_second + anchor_second)[:, None] + corner // 2 % 2) * blocks_third
    block_index = block_index + anchor_third[:, None] + corner % 2
    trainer_key = group * N_GX + owners
    totals = jax.ops.segment_sum(alive_mask.astype(jnp.float32), trainer_key, num_segments=DEVICES)
    patch_weight = 1.0 / jnp.maximum(totals, 1.0)[trainer_key]
    keep = jnp.argsort(jnp.logical_not(alive_mask).astype(jnp.int32), stable=True)[:DEVICES * PICK_MEAN]
    chosen = block_index[keep].reshape(-1)
    inputs = first_rows[chosen]
    targets = target_rows[chosen]
    row_weight = jnp.repeat(patch_weight[keep], 8)
    grad_flat = gradient(inputs, targets, row_weight, w_in, w_mid, w_out)
    direction = adam_direction(moment_one, moment_two, grad_flat)
    return (velocity_next, direction)
```

```python
import math

import jax
import jax.numpy as jnp
from jax import lax
from jax.experimental import pallas as pl
from jax.experimental.pallas import tpu as pltpu
from jax.sharding import PartitionSpec as P

ADAM_STEP = 10
TIME_STEP = 0.2
VISCOSITY = 0.05
BETA_ONE = 0.9
BETA_TWO = 0.999
EPSILON = 1e-08
MESH = pl.DeviceIdType.MESH
F32 = jnp.float32
BF16 = jnp.bfloat16
NN = (((1,), (0,)), ((), ()))
NT = (((1,), (1,)), ((), ()))
TN = (((0,), (0,)), ((), ()))
GELU_K = math.sqrt(2.0 / math.pi)
GELU_C = 0.044715
ROWS = 144
WIDE = 1536


def dot(a, b, dims=NN):
    return lax.dot_general(a, b, dims, preferred_element_type=F32)


def gelu(a):
    t = jnp.tanh(GELU_K * (a + GELU_C * (a * a * a)))
    return a * (0.5 * (1.0 + t))


def gelu_and_slope(a):
    a2 = a * a
    t = jnp.tanh(GELU_K * (a + GELU_C * (a2 * a)))
    cdf = 0.5 * (1.0 + t)
    slope = cdf + (0.5 * GELU_K) * a * (1.0 - t * t) * (1.0 + (3.0 * GELU_C) * a2)
    return a * cdf, slope


def place(r, z, yh, x, yl):
    return {"role": r, "gx": z * 2 + yh, "gy": x * 2 + yl}


def kernel(
    vel_hbm, tgt_hbm, win_hbm, wmid_hbm, wout_hbm, mom1, mom2, picks, owners, counts,
    next_hbm, direction,
    vp, sp, vnext, tgt, w_in, w_mid, w_out, w_first, w_last, perm,
    t_zero, t_one, xf, xb, yf, info, weight, hist_out, hist, ysend, yrecv,
    xs, ys, slope_one, slope_two, h_one, h_two, e_all, b_two, b_one,
    grad, rx, ry, rz, sx, sy, sz, rx2, ry2, rz2, sxy, sz2, rxy3, rz3,
    load_sem, send_sem, recv_sem,
):
    r = lax.axis_index("role")
    i = lax.axis_index("gx")
    j = lax.axis_index("gy")
    z, yh, x, yl = i // 2, i % 2, j // 2, j % 2
    y = yh * 2 + yl
    q = r * 8 + j

    def at_q(k):
        k = lax.rem(k + 16, 16)
        return {"role": k // 8, "gx": i, "gy": k % 8}

    def at_i(k):
        return {"role": r, "gx": lax.rem(k + 16, 16), "gy": j}

    def along_x(d):
        return place(r, z, yh, lax.rem(x + d, 4), yl)

    def along_y(d):
        k = lax.rem(y + d, 4)
        return place(r, z, k // 2, x, k % 2)

    def along_z(d):
        return place(r, lax.rem(z + d, 8), yh, x, yl)

    pair = {"role": 1 - r, "gx": i, "gy": j}

    loads = []

    def load(src, dst):
        c = pltpu.make_async_copy(src, dst, load_sem.at[len(loads)])
        c.start()
        loads.append(c)
        return c

    load_v = load(vel_hbm, vp.at[:, 1:25, 8:32, :])
    load_t = load(tgt_hbm, tgt)
    load_wi = load(win_hbm, w_in)
    load_wo = load(wout_hbm, w_out)
    load_wm = load(wmid_hbm, w_mid)

    barrier = pltpu.get_barrier_semaphore()
    other = at_q(q + 2 * yl - 1)
    for d in range(1, 16):
        pl.semaphore_signal(barrier, inc=1, device_id=at_i(i + d), device_id_type=MESH)
    for d in range(1, 4):
        pl.semaphore_signal(barrier, inc=1, device_id=along_x(d), device_id_type=MESH)
    for who in (place(r, z, yh, x, 1 - yl), place(r, z, 1 - yh, x, 1 - yl), pair, other):
        pl.semaphore_signal(barrier, inc=1, device_id=who, device_id_type=MESH)

    def column(row):
        a = lax.broadcasted_iota(jnp.int32, (32, 32), 0)
        b = lax.broadcasted_iota(jnp.int32, (32, 32), 1)
        picked = jnp.where(a == b, jnp.broadcast_to(row, (32, 32)), 0.0)
        return jnp.broadcast_to(jnp.sum(picked, axis=1, keepdims=True), (32, 128))

    o = picks[...]
    one, nil = jnp.ones_like(o), jnp.zeros_like(o)
    over30 = jnp.where(o >= 30, one, nil)
    over15 = jnp.where(o >= 15, one, nil) + over30 + jnp.where(o >= 45, one, nil)
    first_block = (over30 * 3 + (over15 - 2 * over30)) * 16 + (o - 15 * over15)
    info[0] = column(first_block.astype(F32))
    owner = column(owners[...].astype(F32))
    slot = lax.broadcasted_iota(jnp.int32, (32, 128), 0)
    lane = lax.broadcasted_iota(jnp.int32, (32, 128), 1).astype(F32)
    alive = slot < jnp.broadcast_to(counts[...], (32, 128))
    match = jnp.where(alive, jnp.where(lane == owner, 1.0, 0.0), 0.0)
    hist_out[...] = jnp.broadcast_to(jnp.sum(match, axis=0, keepdims=True), (8, 128))
    hist[pl.ds(i, 1)] = hist_out[...].reshape(1, 8, 128)

    count = [0]

    def send(src, dst, who):
        k = count[0]
        count[0] += 1
        c = pltpu.make_async_remote_copy(
            src_ref=src, dst_ref=dst, send_sem=send_sem.at[k], recv_sem=recv_sem.at[k],
            device_id=who, device_id_type=MESH,
        )
        c.start()
        return c

    pl.semaphore_wait(barrier, 22)

    hist_copies = [send(hist_out, hist.at[i], at_i(i + d)) for d in range(1, 16)]
    pair_info = send(info.at[0], info.at[1], pair)

    def halo_start(field, slot):
        flat = field.reshape(3 * 26 * 40, 128)
        for c in range(3):
            ysend[slot, 0, c] = flat[pl.ds((c * 26 + 1) * 40 + 8, 24, stride=40), :]
            ysend[slot, 1, c] = flat[pl.ds((c * 26 + 1) * 40 + 31, 24, stride=40), :]
        return [
            send(field.at[:, 1, 8:32, :], field.at[:, 25, 8:32, :], at_i(i - 1)),
            send(field.at[:, 24, 8:32, :], field.at[:, 0, 8:32, :], at_i(i + 1)),
            send(ysend.at[slot, 0], yrecv.at[slot, 1], at_q(q - 1)),
            send(ysend.at[slot, 1], yrecv.at[slot, 0], at_q(q + 1)),
        ]

    def halo_finish(field, slot, copies):
        for c in copies:
            c.wait_recv()
        flat = field.reshape(3 * 26 * 40, 128)
        for c in range(3):
            flat[pl.ds((c * 26 + 1) * 40 + 7, 24, stride=40), :] = yrecv[slot, 0, c]
            flat[pl.ds((c * 26 + 1) * 40 + 32, 24, stride=40), :] = yrecv[slot, 1, c]

    def turn(take):
        def body(k, carry):
            d = take(k // 3, k % 3).reshape(192, 128)
            rows = pl.ds(pl.multiple_of(k * 128, 128), 128)
            t_zero[rows, :] = d[:128].T
            t_one[rows, 0:64] = d[128:].T
            return carry

        lax.fori_loop(0, 9, body, 0)

    def take_from(field):
        def take(bx, by):
            return field[:, pl.ds(bx * 8 + 1, 8), pl.ds(pl.multiple_of(by * 8 + 8, 8), 8), :]

        return take

    half = lax.broadcasted_iota(jnp.int32, (ROWS, 128), 1)

    def rows_of(write):
        for oz in range(8):
            write(oz * 128, t_zero[pl.ds(oz, ROWS, stride=8), :])
        for k in range(4):
            a = t_one[pl.ds(2 * k, ROWS, stride=8), :]
            b = t_one[pl.ds(2 * k + 1, ROWS, stride=8), :]
            write(1024 + k * 128, jnp.where(half < 64, a, pltpu.roll(b, 64, 1)))

    pr = lax.broadcasted_iota(jnp.int32, (256, 256), 0)
    pc = lax.broadcasted_iota(jnp.int32, (256, 256), 1)
    perm[...] = jnp.where(pc == (pr & 31) * 8 + (pr >> 5), 1.0, 0.0).astype(BF16)

    load_t.wait()

    def take_target(bx, by):
        return tgt[:, pl.ds(bx * 8, 8), pl.ds(pl.multiple_of(by * 8, 8), 8), :]

    turn(take_target)
    for g in range(6):
        tiles = []
        src, base = (t_zero, g) if g < 4 else (t_one, g - 4)
        for quad in range(2):
            tile = None
            for m in range(4):
                part = src[pl.ds(4 * quad + m, ROWS, stride=8), :]
                shift = (32 * (m - base)) % 128
                if shift:
                    part = pltpu.roll(part, shift, 1)
                tile = part if tile is None else jnp.where(half >= 32 * m, part, tile)
            tiles.append(tile.astype(BF16))
        yf[0, :, 256 * g : 256 * g + 256] = dot(jnp.concatenate(tiles, axis=1), perm[...])
    pair_y = send(yf.at[0], yf.at[1], pair)

    load_v.wait()
    halo_one = halo_start(vp, 0)
    turn(take_from(vp))

    def write_x(at, tile):
        xf[0, :, at : at + 128] = tile
        xb[0, :, at : at + 128] = tile.astype(BF16)

    rows_of(write_x)
    pair_x = send(xf.at[0], xf.at[1], pair)

    for c in hist_copies:
        c.wait_recv()
    totals = jnp.sum(hist[...], axis=0)
    inverse = 1.0 / jnp.maximum(totals, 1.0)
    own_weight = jnp.sum(match * inverse[0:1, :], axis=1, keepdims=True)
    weight[0] = jnp.broadcast_to(own_weight, (32, 128))
    pair_w = send(weight.at[0], weight.at[1], pair)

    load_wi.wait()
    load_wo.wait()
    load_wm.wait()
    for g in range(6):
        wi = dot(perm[...], w_in[256 * g : 256 * g + 256, :]).astype(BF16)
        wo = dot(perm[...], w_out[:, 256 * g : 256 * g + 256], NT).astype(BF16)
        for oz in range(8):
            at = oz * 128 + 32 * g if g < 4 else 1024 + oz * 64 + 32 * (g - 4)
            w_first[at : at + 32, :] = wi[32 * oz : 32 * oz + 32]
            w_last[at : at + 32, :] = wo[32 * oz : 32 * oz + 32]

    for c in (pair_info, pair_y, pair_x, pair_w):
        c.wait_recv()

    def side(s, carry):
        rows = pl.ds(pl.multiple_of(s * 256, 256), 256)

        @pl.when(s == 1)
        def _():
            xb[1] = xf[1].astype(BF16)

        start = info[s]
        start = jnp.concatenate([start, start], axis=1)[:, :ROWS]
        block = lax.broadcasted_iota(jnp.int32, (32, ROWS), 1).astype(F32)
        chosen = jnp.concatenate(
            [
                jnp.where(block == start + float(k // 4 * 48 + k // 2 % 2 * 16 + k % 2), 1.0, 0.0)
                for k in range(8)
            ],
            axis=0,
        ).astype(BF16)
        for n in range(3):
            cols = slice(512 * n, 512 * n + 512)
            xs[rows, cols] = dot(chosen, xb[s, :, cols]).astype(BF16)
        a, slope = gelu_and_slope(dot(xs[rows, :], w_first[...]))
        slope_one[rows, :] = slope
        h1 = a.astype(BF16)
        h_one[rows, :] = h1
        a, slope = gelu_and_slope(dot(h1, w_mid[...]))
        h2 = a.astype(BF16)
        h_two[rows, :] = h2
        w8 = 2.0 * jnp.concatenate([weight[s]] * 8, axis=0)
        w8 = jnp.concatenate([w8] * 4, axis=1)
        up = None
        for n in range(3):
            cols = slice(512 * n, 512 * n + 512)
            target = dot(chosen, yf[s, :, cols].astype(BF16))
            e = (w8 * (dot(h2, w_out[:, cols]) - target)).astype(BF16)
            e_all[rows, cols] = e
            part = dot(e, w_out[:, cols], NT)
            up = part if up is None else up + part
        b_two[rows, :] = (slope * up).astype(BF16)
        return carry

    lax.fori_loop(0, 2, side, 0)

    def put(value, start, stride, size):
        for cb in range(value.shape[1] // 128):
            grad_flat[pl.ds(start + cb, size, stride=stride), :] = value[:, cb * 128 : cb * 128 + 128]

    grad_flat = grad.reshape(7168, 128)

    @pl.when(r == 0)
    def _():
        for s in range(2):
            rows = slice(256 * s, 256 * s + 256)
            up = dot(b_two[rows, :], w_mid[...], NT)
            b_one[rows, :] = (slope_one[rows, :] * up).astype(BF16)
        for k in range(4):
            part = dot(xs[:, 256 * k : 256 * k + 256], b_one[...], TN)
            put(part[:128], 8 * k, 32, 128)
            put(part[128:], 8 * k + 4, 32, 128)
        for k in range(2):
            part = dot(xs[:, 1024 + 256 * k : 1280 + 256 * k], b_one[...], TN)
            for m in range(4):
                put(part[64 * m : 64 * m + 64], 4096 + 4 * (4 * k + m), 32, 64)
        put(dot(h_one[:, 0:256], b_two[...], TN), 6144, 4, 256)

    @pl.when(r == 1)
    def _():
        for k in range(2):
            for n in range(3):
                part = dot(h_two[:, 256 * k : 256 * k + 256], e_all[:, 512 * n : 512 * n + 512], TN)
                put(part, 1024 + 3072 * k + 4 * n, 12, 256)
        put(dot(h_one[:, 256:512], b_two[...], TN), 0, 4, 256)

    gx5 = grad.reshape(16, 4, 2, 56, 128)
    gy6 = grad.reshape(8, 2, 4, 2, 56, 128)
    gz = grad.reshape(8, 16, 56, 128)
    copies_x, copies_y, copies_z = [], [], []
    for d in range(1, 4):
        copies_x.append(send(gx5.at[:, lax.rem(x + d, 4), :, 0:24, :], rx.at[d - 1], along_x(d)))
        k = lax.rem(y + d, 4)
        copies_y.append(send(gy6.at[:, k // 2, :, k % 2, 24:48, :], ry.at[d - 1], along_y(d)))
    for d in range(1, 8):
        copies_z.append(send(gz.at[lax.rem(z + d, 8), :, 48:56, :], rz.at[d - 1], along_z(d)))

    def closure(rows):
        q1 = gelu(dot(rows, w_first[...])).astype(BF16)
        q2 = gelu(dot(q1, w_mid[...])).astype(BF16)
        for n in range(2):
            out = dot(q2, w_last[512 * n : 512 * n + 512, :], NT)
            for m in range(4):
                t_zero[pl.ds(4 * n + m, ROWS, stride=8), :] = out[:, 128 * m : 128 * m + 128]
        out = dot(q2, w_last[1024:1536, :], NT)
        for m in range(4):
            tile = out[:, 128 * m : 128 * m + 128]
            t_one[pl.ds(2 * m, ROWS, stride=8), :] = tile
            t_one[pl.ds(2 * m + 1, ROWS, stride=8), :] = pltpu.roll(tile, 64, 1)

    def section(field, finish):
        def body(k, carry):
            bx, by = k // 3, k % 3
            rows = pl.ds(pl.multiple_of(k * 128, 128), 128)
            closed = [None, None, None]
            front = t_zero[rows, :].T
            closed[0] = front[:64].reshape(8, 8, 128)
            closed[1] = front[64:].reshape(8, 8, 128)
            closed[2] = t_one[rows, :].T[:64].reshape(8, 8, 128)
            here = pl.ds(pl.multiple_of(by * 8 + 8, 8), 8)
            around = pl.ds(pl.multiple_of(by * 8, 8), 24)
            center = [field[c, pl.ds(bx * 8 + 1, 8), here, :] for c in range(3)]
            for c in range(3):
                mid = center[c]
                first_up = field[c, pl.ds(bx * 8 + 2, 8), here, :]
                first_down = field[c, pl.ds(bx * 8, 8), here, :]
                window = field[c, pl.ds(bx * 8 + 1, 8), around, :]
                second_up = window[:, 9:17, :]
                second_down = window[:, 7:15, :]
                third_up = pltpu.roll(mid, 127, 2)
                third_down = pltpu.roll(mid, 1, 2)
                advect = (
                    center[0] * ((first_up - first_down) * 0.5)
                    + center[1] * ((second_up - second_down) * 0.5)
                    + center[2] * ((third_up - third_down) * 0.5)
                )
                spread = (
                    first_up + first_down + (second_up + second_down) + (third_up + third_down) - 6.0 * mid
                )
                finish(c, bx, by, mid, VISCOSITY * spread - advect + closed[c])
            return carry

        lax.fori_loop(0, 9, body, 0)

    halo_finish(vp, 0, halo_one)
    closure(xb[0])

    def finish_one(c, bx, by, mid, rate):
        here = pl.ds(pl.multiple_of(by * 8 + 8, 8), 8)
        sp[c, pl.ds(bx * 8 + 1, 8), here, :] = mid + TIME_STEP * rate

    section(vp, finish_one)
    halo_two = halo_start(sp, 1)
    turn(take_from(sp))

    def write_second(at, tile):
        xb[1, :, at : at + 128] = tile.astype(BF16)

    rows_of(write_second)
    closure(xb[1])
    halo_finish(sp, 1, halo_two)

    def finish_two(c, bx, by, mid, rate):
        here = pl.ds(pl.multiple_of(by * 8 + 8, 8), 8)
        start = vp[c, pl.ds(bx * 8 + 1, 8), here, :]
        vnext[c, pl.ds(bx * 8, 8), pl.ds(pl.multiple_of(by * 8, 8), 8), :] = 0.75 * start + 0.25 * (
            mid + TIME_STEP * rate
        )

    section(sp, finish_two)
    store = pltpu.make_async_copy(vnext, next_hbm, load_sem.at[5])
    store.start()

    for c in copies_x:
        c.wait_recv()
    for k in range(16):
        sx[k] = gx5[k, x, :, 0:24, :] + (rx[0, k] + rx[1, k] + rx[2, k])
    sx6 = sx.reshape(8, 2, 2, 24, 128)
    next_x, next_y, next_z = [], [], []
    for d in range(1, 4):
        k = lax.rem(y + d, 4)
        next_x.append(send(sx6.at[:, k // 2, k % 2], rx2.at[d - 1], along_y(d)))
    for c in copies_y:
        c.wait_recv()
    for k in range(8):
        sy[k] = gy6[k, yh, :, yl, 24:48, :] + (ry[0, k] + ry[1, k] + ry[2, k])
    for d in range(1, 4):
        next_y.append(send(sy.at[:, lax.rem(x + d, 4)], ry2.at[d - 1], along_x(d)))
    for c in copies_z:
        c.wait_recv()
    total = gz[z, :, 48:56, :]
    for d in range(7):
        total = total + rz[d]
    sz[...] = total.reshape(2, 4, 2, 8, 128)
    for d in range(1, 4):
        next_z.append(send(sz.at[:, lax.rem(x + d, 4)], rz2.at[d - 1], along_x(d)))

    for c in next_x:
        c.wait_recv()
    for k in range(8):
        sxy[k, 0:24, :] = sx6[k, yh, yl] + (rx2[0, k] + rx2[1, k] + rx2[2, k])
    for c in next_y:
        c.wait_recv()
    for k in range(8):
        sxy[k, 24:48, :] = sy[k, x] + (ry2[0, k] + ry2[1, k] + ry2[2, k])
    last = [send(sxy.at[lax.rem(z + d, 8)], rxy3.at[d - 1], along_z(d)) for d in range(1, 8)]
    for c in next_z:
        c.wait_recv()
    sz2[...] = sz[:, x] + (rz2[0] + rz2[1] + rz2[2])
    last_z = []
    for d in range(1, 4):
        k = lax.rem(y + d, 4)
        last_z.append(send(sz2.at[k // 2, k % 2], rz3.at[d - 1], along_y(d)))
    for c in last + last_z:
        c.wait_recv()
    front = sxy[z]
    for d in range(7):
        front = front + rxy3[d]
    back = sz2[yh, yl] + (rz3[0] + rz3[1] + rz3[2])
    g = jnp.concatenate([front, back], axis=0)
    moment = BETA_ONE * mom1[...] + (1.0 - BETA_ONE) * g
    second = BETA_TWO * mom2[...] + (1.0 - BETA_TWO) * g * g
    corrected = moment / (1.0 - BETA_ONE**ADAM_STEP)
    direction[...] = corrected / (jnp.sqrt(second / (1.0 - BETA_TWO**ADAM_STEP)) + EPSILON)

    for c in (
        hist_copies + [pair_info, pair_y, pair_x, pair_w] + halo_one + halo_two
        + copies_x + copies_y + copies_z + next_x + next_y + next_z + last + last_z
    ):
        c.wait_send()
    store.wait()


def local(velocity, target_field, w_in, w_mid, w_out, moment_one, moment_two, picks, owners, counts):
    any_space = pl.BlockSpec(memory_space=pl.ANY)
    vmem = pl.BlockSpec(memory_space=pltpu.VMEM)
    V = pltpu.VMEM
    next_velocity, direction = pl.pallas_call(
        kernel,
        out_shape=(
            jax.ShapeDtypeStruct(velocity.shape, F32),
            jax.ShapeDtypeStruct((56, 128), F32),
        ),
        in_specs=[any_space] * 5 + [vmem] * 5,
        out_specs=(any_space, vmem),
        scratch_shapes=[
            V((3, 26, 40, 128), F32),
            V((3, 26, 40, 128), F32),
            V((3, 24, 24, 128), F32),
            V((3, 24, 24, 128), F32),
            V((1536, 512), BF16),
            V((512, 512), BF16),
            V((512, 1536), BF16),
            V((1536, 512), BF16),
            V((1536, 512), BF16),
            V((256, 256), BF16),
            V((1152, 128), F32),
            V((1152, 128), F32),
            V((2, ROWS, WIDE), F32),
            V((2, ROWS, WIDE), BF16),
            V((2, ROWS, WIDE), F32),
            V((2, 32, 128), F32),
            V((2, 32, 128), F32),
            V((8, 128), F32),
            V((16, 8, 128), F32),
            V((2, 2, 3, 24, 128), F32),
            V((2, 2, 3, 24, 128), F32),
            V((512, WIDE), BF16),
            V((8, 128), BF16),
            V((512, 512), F32),
            V((8, 128), F32),
            V((512, 512), BF16),
            V((512, 512), BF16),
            V((512, WIDE), BF16),
            V((512, 512), BF16),
            V((512, 512), BF16),
            V((7168, 128), F32),
            V((3, 16, 2, 24, 128), F32),
            V((3, 8, 4, 24, 128), F32),
            V((7, 16, 8, 128), F32),
            V((16, 2, 24, 128), F32),
            V((8, 4, 24, 128), F32),
            V((2, 4, 2, 8, 128), F32),
            V((3, 8, 24, 128), F32),
            V((3, 8, 24, 128), F32),
            V((3, 2, 2, 8, 128), F32),
            V((8, 48, 128), F32),
            V((2, 2, 8, 128), F32),
            V((7, 48, 128), F32),
            V((3, 8, 128), F32),
            pltpu.SemaphoreType.DMA((6,)),
            pltpu.SemaphoreType.DMA((60,)),
            pltpu.SemaphoreType.DMA((60,)),
        ],
        compiler_params=pltpu.CompilerParams(
            collective_id=0, has_side_effects=True, vmem_limit_bytes=60 * 2**20
        ),
    )(
        velocity, target_field, w_in, w_mid, w_out,
        moment_one.reshape(56, 128), moment_two.reshape(56, 128),
        picks.reshape(1, 32), owners.reshape(1, 32), counts,
    )
    return next_velocity, direction.reshape(7168)


def solution(mesh):
    return jax.shard_map(
        local,
        mesh=mesh,
        in_specs=(
            P(None, "gx", ("role", "gy"), None),
            P(None, "gx", ("role", "gy"), None),
            P(),
            P(),
            P(),
            P(("role", "gx", "gy")),
            P(("role", "gx", "gy")),
            P(("role", "gx", "gy")),
            P(("role", "gx", "gy")),
            P(("role", "gy"), "gx"),
        ),
        out_specs=(P(None, "gx", ("role", "gy"), None), P(("role", "gx", "gy"))),
        check_vma=False,
    )
```

```python
import math

import jax
import jax.numpy as jnp
from jax import lax
from jax.experimental import pallas as pl
from jax.experimental.pallas import tpu as pltpu
from jax.sharding import PartitionSpec as P

ADAM_STEP = 10
TIME_STEP = 0.2
VISCOSITY = 0.05
BETA_ONE = 0.9
BETA_TWO = 0.999
EPSILON = 1e-08
MESH = pl.DeviceIdType.MESH
F32 = jnp.float32
BF16 = jnp.bfloat16
NN = (((1,), (0,)), ((), ()))
NT = (((1,), (1,)), ((), ()))
TN = (((0,), (0,)), ((), ()))
GELU_K = math.sqrt(2.0 / math.pi)
GELU_C = 0.044715
ROWS = 144
WIDE = 1536


def dot(a, b, dims=NN):
    return lax.dot_general(a, b, dims, preferred_element_type=F32)


def gelu(a):
    t = jnp.tanh(GELU_K * (a + GELU_C * (a * a * a)))
    return a * (0.5 * (1.0 + t))


def gelu_and_slope(a):
    a2 = a * a
    t = jnp.tanh(GELU_K * (a + GELU_C * (a2 * a)))
    cdf = 0.5 * (1.0 + t)
    slope = cdf + (0.5 * GELU_K) * a * (1.0 - t * t) * (1.0 + (3.0 * GELU_C) * a2)
    return a * cdf, slope


def place(r, z, yh, x, yl):
    return {"role": r, "gx": z * 2 + yh, "gy": x * 2 + yl}


def kernel(
    vel_hbm, tgt_hbm, win_hbm, wmid_hbm, wout_hbm, mom1, mom2, picks, owners, counts,
    vnext, direction,
    vp, sp, tgt, w_in, w_mid, w_out, w_first, w_last, perm,
    t_zero, t_one, xf, xb, yf, info, weight, hist_out, hist, ysend, yrecv,
    xs, slope_one, slope_two, h_one, h_two, e_all, b_two, b_one,
    grad, rx, ry, rz, sx, sy, sz, rx2, ry2, rz2, sxy, sz2, rxy3, rz3,
    rxs, rys, sxs, syt, rx2s, ry2s, sxys, rxy3s,
    load_sem, send_sem, recv_sem,
):
    r = lax.axis_index("role")
    i = lax.axis_index("gx")
    j = lax.axis_index("gy")
    z, yh, x, yl = i // 2, i % 2, j // 2, j % 2
    y = yh * 2 + yl
    q = r * 8 + j

    def at_q(k):
        k = lax.rem(k + 16, 16)
        return {"role": k // 8, "gx": i, "gy": k % 8}

    def at_i(k):
        return {"role": r, "gx": lax.rem(k + 16, 16), "gy": j}

    def along_x(d):
        return place(r, z, yh, lax.rem(x + d, 4), yl)

    def along_y(d):
        k = lax.rem(y + d, 4)
        return place(r, z, k // 2, x, k % 2)

    def along_z(d):
        return place(r, lax.rem(z + d, 8), yh, x, yl)

    pair = {"role": 1 - r, "gx": i, "gy": j}

    loads = []

    def load(src, dst):
        c = pltpu.make_async_copy(src, dst, load_sem.at[len(loads)])
        c.start()
        loads.append(c)
        return c

    load_v = load(vel_hbm, vp.at[:, 1:25, 8:32, :])
    load_t = load(tgt_hbm, tgt)
    load_wi = load(win_hbm, w_in)
    load_wo = load(wout_hbm, w_out)
    load_wm = load(wmid_hbm, w_mid)

    barrier = pltpu.get_barrier_semaphore()
    other = at_q(q + 2 * yl - 1)
    for d in range(1, 16):
        pl.semaphore_signal(barrier, inc=1, device_id=at_i(i + d), device_id_type=MESH)
    for d in range(1, 4):
        pl.semaphore_signal(barrier, inc=1, device_id=along_x(d), device_id_type=MESH)
    for who in (place(r, z, yh, x, 1 - yl), place(r, z, 1 - yh, x, 1 - yl), pair, other):
        pl.semaphore_signal(barrier, inc=1, device_id=who, device_id_type=MESH)

    def column(row):
        a = lax.broadcasted_iota(jnp.int32, (32, 32), 0)
        b = lax.broadcasted_iota(jnp.int32, (32, 32), 1)
        picked = jnp.where(a == b, jnp.broadcast_to(row, (32, 32)), 0.0)
        return jnp.broadcast_to(jnp.sum(picked, axis=1, keepdims=True), (32, 128))

    o = picks[...]
    one, nil = jnp.ones_like(o), jnp.zeros_like(o)
    over30 = jnp.where(o >= 30, one, nil)
    over15 = jnp.where(o >= 15, one, nil) + over30 + jnp.where(o >= 45, one, nil)
    first_block = (over30 * 3 + (over15 - 2 * over30)) * 16 + (o - 15 * over15)
    info[0] = column(first_block.astype(F32))
    owner = column(owners[...].astype(F32))
    slot = lax.broadcasted_iota(jnp.int32, (32, 128), 0)
    lane = lax.broadcasted_iota(jnp.int32, (32, 128), 1).astype(F32)
    alive = slot < jnp.broadcast_to(counts[...], (32, 128))
    match = jnp.where(alive, jnp.where(lane == owner, 1.0, 0.0), 0.0)
    hist_out[...] = jnp.broadcast_to(jnp.sum(match, axis=0, keepdims=True), (8, 128))
    hist[pl.ds(i, 1)] = hist_out[...].reshape(1, 8, 128)

    count = [0]

    def send(src, dst, who):
        k = count[0]
        count[0] += 1
        c = pltpu.make_async_remote_copy(
            src_ref=src, dst_ref=dst, send_sem=send_sem.at[k], recv_sem=recv_sem.at[k],
            device_id=who, device_id_type=MESH,
        )
        c.start()
        return c

    def halo_start(field, slot):
        flat = field.reshape(3 * 26 * 40, 128)
        for c in range(3):
            ysend[slot, 0, c] = flat[pl.ds((c * 26 + 1) * 40 + 8, 24, stride=40), :]
            ysend[slot, 1, c] = flat[pl.ds((c * 26 + 1) * 40 + 31, 24, stride=40), :]
        return [
            send(field.at[:, 1, 8:32, :], field.at[:, 25, 8:32, :], at_i(i - 1)),
            send(field.at[:, 24, 8:32, :], field.at[:, 0, 8:32, :], at_i(i + 1)),
            send(ysend.at[slot, 0], yrecv.at[slot, 1], at_q(q - 1)),
            send(ysend.at[slot, 1], yrecv.at[slot, 0], at_q(q + 1)),
        ]

    def halo_finish(field, slot, copies):
        for c in copies:
            c.wait_recv()
        flat = field.reshape(3 * 26 * 40, 128)
        for c in range(3):
            flat[pl.ds((c * 26 + 1) * 40 + 7, 24, stride=40), :] = yrecv[slot, 0, c]
            flat[pl.ds((c * 26 + 1) * 40 + 32, 24, stride=40), :] = yrecv[slot, 1, c]

    def turn(take):
        def body(k, carry):
            d = take(k // 3, k % 3).reshape(192, 128)
            rows = pl.ds(pl.multiple_of(k * 128, 128), 128)
            t_zero[rows, :] = d[:128].T
            t_one[rows, 0:64] = d[128:].T
            return carry

        lax.fori_loop(0, 9, body, 0)

    def take_from(field):
        def take(bx, by):
            return field[:, pl.ds(bx * 8 + 1, 8), pl.ds(pl.multiple_of(by * 8 + 8, 8), 8), :]

        return take

    half = lax.broadcasted_iota(jnp.int32, (ROWS, 128), 1)

    def rows_of(write):
        for oz in range(8):
            write(oz * 128, t_zero[pl.ds(oz, ROWS, stride=8), :])
        for k in range(4):
            a = t_one[pl.ds(2 * k, ROWS, stride=8), :]
            b = t_one[pl.ds(2 * k + 1, ROWS, stride=8), :]
            write(1024 + k * 128, jnp.where(half < 64, a, pltpu.roll(b, 64, 1)))

    pr = lax.broadcasted_iota(jnp.int32, (256, 256), 0)
    pc = lax.broadcasted_iota(jnp.int32, (256, 256), 1)
    perm[...] = jnp.where(pc == (pr & 31) * 8 + (pr >> 5), 1.0, 0.0).astype(BF16)

    pl.semaphore_wait(barrier, 22)
    hist_copies = [send(hist_out, hist.at[i], at_i(i + d)) for d in range(1, 16)]
    pair_info = send(info.at[0], info.at[1], pair)

    load_v.wait()
    turn(take_from(vp))

    def write_x(at, tile):
        xf[0, :, at : at + 128] = tile
        xb[0, :, at : at + 128] = tile.astype(BF16)

    rows_of(write_x)

    pair_x = send(xf.at[0], xf.at[1], pair)
    halo_one = halo_start(vp, 0)

    load_t.wait()

    def take_target(bx, by):
        return tgt[:, pl.ds(bx * 8, 8), pl.ds(pl.multiple_of(by * 8, 8), 8), :]

    turn(take_target)
    for g in range(6):
        tiles = []
        src, base = (t_zero, g) if g < 4 else (t_one, g - 4)
        for quad in range(2):
            tile = None
            for m in range(4):
                part = src[pl.ds(4 * quad + m, ROWS, stride=8), :]
                shift = (32 * (m - base)) % 128
                if shift:
                    part = pltpu.roll(part, shift, 1)
                tile = part if tile is None else jnp.where(half >= 32 * m, part, tile)
            tiles.append(tile.astype(BF16))
        yf[0, :, 256 * g : 256 * g + 256] = dot(jnp.concatenate(tiles, axis=1), perm[...])
    pair_y = send(yf.at[0], yf.at[1], pair)

    def block_order(g, value, dst):
        for oz in range(8):
            at = oz * 128 + 32 * g if g < 4 else 1024 + oz * 64 + 32 * (g - 4)
            dst[at : at + 32, :] = value[32 * oz : 32 * oz + 32].astype(BF16)

    load_wi.wait()
    for g in range(6):
        block_order(g, dot(perm[...], w_in[256 * g : 256 * g + 256, :]), w_first)

    def choose(s):
        start = info[s]
        start = jnp.concatenate([start, start], axis=1)[:, :ROWS]
        block = lax.broadcasted_iota(jnp.int32, (32, ROWS), 1).astype(F32)
        return jnp.concatenate(
            [
                jnp.where(block == start + float(k // 4 * 48 + k // 2 % 2 * 16 + k % 2), 1.0, 0.0)
                for k in range(8)
            ],
            axis=0,
        ).astype(BF16)

    def forward(s):
        rows = slice(256 * s, 256 * s + 256)
        chosen = choose(s)
        for n in range(3):
            cols = slice(512 * n, 512 * n + 512)
            xs[rows, cols] = dot(chosen, xb[s, :, cols]).astype(BF16)
        a, slope = gelu_and_slope(dot(xs[rows, :], w_first[...]))
        slope_one[rows, :] = slope
        h1 = a.astype(BF16)
        h_one[rows, :] = h1
        a, slope = gelu_and_slope(dot(h1, w_mid[...]))
        slope_two[rows, :] = slope
        h_two[rows, :] = a.astype(BF16)

    def backward(s):
        rows = slice(256 * s, 256 * s + 256)
        chosen = choose(s)
        w8 = 2.0 * jnp.concatenate([weight[s]] * 8, axis=0)
        w8 = jnp.concatenate([w8] * 4, axis=1)
        up = None
        for n in range(3):
            cols = slice(512 * n, 512 * n + 512)
            target = dot(chosen, yf[s, :, cols].astype(BF16))
            e = (w8 * (dot(h_two[rows, :], w_out[:, cols]) - target)).astype(BF16)
            e_all[rows, cols] = e
            part = dot(e, w_out[:, cols], NT)
            up = part if up is None else up + part
        b_two[rows, :] = (slope_two[rows, :] * up).astype(BF16)

    def closure(rows):
        q1 = gelu(dot(rows, w_first[...])).astype(BF16)
        q2 = gelu(dot(q1, w_mid[...])).astype(BF16)
        for n in range(2):
            out = dot(q2, w_last[512 * n : 512 * n + 512, :], NT)
            for m in range(4):
                t_zero[pl.ds(4 * n + m, ROWS, stride=8), :] = out[:, 128 * m : 128 * m + 128]
        out = dot(q2, w_last[1024:1536, :], NT)
        for m in range(4):
            tile = out[:, 128 * m : 128 * m + 128]
            t_one[pl.ds(2 * m, ROWS, stride=8), :] = tile
            t_one[pl.ds(2 * m + 1, ROWS, stride=8), :] = pltpu.roll(tile, 64, 1)

    def section(field, finish):
        def body(k, carry):
            bx, by = k // 3, k % 3
            rows = pl.ds(pl.multiple_of(k * 128, 128), 128)
            closed = [None, None, None]
            front = t_zero[rows, :].T
            closed[0] = front[:64].reshape(8, 8, 128)
            closed[1] = front[64:].reshape(8, 8, 128)
            closed[2] = t_one[rows, :].T[:64].reshape(8, 8, 128)
            here = pl.ds(pl.multiple_of(by * 8 + 8, 8), 8)
            around = pl.ds(pl.multiple_of(by * 8, 8), 24)
            center = [field[c, pl.ds(bx * 8 + 1, 8), here, :] for c in range(3)]
            for c in range(3):
                mid = center[c]
                first_up = field[c, pl.ds(bx * 8 + 2, 8), here, :]
                first_down = field[c, pl.ds(bx * 8, 8), here, :]
                window = field[c, pl.ds(bx * 8 + 1, 8), around, :]
                second_up = window[:, 9:17, :]
                second_down = window[:, 7:15, :]
                third_up = pltpu.roll(mid, 127, 2)
                third_down = pltpu.roll(mid, 1, 2)
                advect = (
                    center[0] * ((first_up - first_down) * 0.5)
                    + center[1] * ((second_up - second_down) * 0.5)
                    + center[2] * ((third_up - third_down) * 0.5)
                )
                spread = (
                    first_up + first_down + (second_up + second_down) + (third_up + third_down) - 6.0 * mid
                )
                finish(c, bx, by, mid, VISCOSITY * spread - advect + closed[c])
            return carry

        lax.fori_loop(0, 9, body, 0)

    load_wm.wait()
    load_wo.wait()
    forward(0)
    pair_info.wait_recv()
    pair_x.wait_recv()
    xb[1] = xf[1].astype(BF16)
    forward(1)

    for c in hist_copies:
        c.wait_recv()
    totals = jnp.sum(hist[...], axis=0)
    inverse = 1.0 / jnp.maximum(totals, 1.0)
    own_weight = jnp.sum(match * inverse[0:1, :], axis=1, keepdims=True)
    weight[0] = jnp.broadcast_to(own_weight, (32, 128))
    pair_w = send(weight.at[0], weight.at[1], pair)

    backward(0)
    pair_y.wait_recv()
    pair_w.wait_recv()
    backward(1)

    def put(value, start, stride, size):
        for cb in range(value.shape[1] // 128):
            grad_flat[pl.ds(start + cb, size, stride=stride), :] = value[:, cb * 128 : cb * 128 + 128]

    grad_flat = grad.reshape(7168, 128)

    @pl.when(r == 0)
    def _():
        for s in range(2):
            rows = slice(256 * s, 256 * s + 256)
            up = dot(b_two[rows, :], w_mid[...], NT)
            b_one[rows, :] = (slope_one[rows, :] * up).astype(BF16)
        for k in range(4):
            part = dot(xs[:, 256 * k : 256 * k + 256], b_one[...], TN)
            put(part[:128], 8 * k, 32, 128)
            put(part[128:], 8 * k + 4, 32, 128)
        for k in range(2):
            part = dot(xs[:, 1024 + 256 * k : 1280 + 256 * k], b_one[...], TN)
            for m in range(4):
                put(part[64 * m : 64 * m + 64], 4096 + 4 * (4 * k + m), 32, 64)
        put(dot(h_one[:, 0:256], b_two[...], TN), 6144, 4, 256)

    @pl.when(r == 1)
    def _():
        for k in range(2):
            for n in range(3):
                part = dot(h_two[:, 256 * k : 256 * k + 256], e_all[:, 512 * n : 512 * n + 512], TN)
                put(part, 1024 + 3072 * k + 4 * n, 12, 256)
        put(dot(h_one[:, 256:512], b_two[...], TN), 0, 4, 256)

    gx5 = grad.reshape(16, 4, 2, 56, 128)
    gy6 = grad.reshape(8, 2, 4, 2, 56, 128)
    gz = grad.reshape(8, 16, 56, 128)
    copies_z = []

    def first_phase(at, size, from_x, from_y):
        to_x, to_y = [], []
        for d in range(1, 4):
            to_x.append(send(gx5.at[:, lax.rem(x + d, 4), :, at : at + size, :], from_x.at[d - 1], along_x(d)))
            k = lax.rem(y + d, 4)
            here = slice(24 + at, 24 + at + size)
            to_y.append(send(gy6.at[:, k // 2, :, k % 2, here, :], from_y.at[d - 1], along_y(d)))
        return to_x, to_y

    big_x, big_y = first_phase(0, 16, rx, ry)
    for d in range(1, 8):
        copies_z.append(send(gz.at[lax.rem(z + d, 8), :, 48:56, :], rz.at[d - 1], along_z(d)))
    small_x, small_y = first_phase(16, 8, rxs, rys)

    for g in range(6):
        block_order(g, dot(perm[...], w_out[:, 256 * g : 256 * g + 256], NT), w_last)
    closure(xb[0])
    halo_finish(vp, 0, halo_one)

    def finish_one(c, bx, by, mid, rate):
        here = pl.ds(pl.multiple_of(by * 8 + 8, 8), 8)
        sp[c, pl.ds(bx * 8 + 1, 8), here, :] = mid + TIME_STEP * rate

    section(vp, finish_one)
    halo_two = halo_start(sp, 1)
    turn(take_from(sp))

    def write_second(at, tile):
        xb[1, :, at : at + 128] = tile.astype(BF16)

    rows_of(write_second)
    closure(xb[1])
    def second_phase(at, size, to_x, to_y, from_x, from_y, sum_x, sum_y, next_x, next_y):
        out_x, out_y = [], []
        for c in to_x:
            c.wait_recv()
        for k in range(16):
            sum_x[k] = gx5[k, x, :, at : at + size, :] + (from_x[0, k] + from_x[1, k] + from_x[2, k])
        view = sum_x.reshape(8, 2, 2, size, 128)
        for d in range(1, 4):
            k = lax.rem(y + d, 4)
            out_x.append(send(view.at[:, k // 2, k % 2], next_x.at[d - 1], along_y(d)))
        for c in to_y:
            c.wait_recv()
        here = slice(24 + at, 24 + at + size)
        for k in range(8):
            sum_y[k] = gy6[k, yh, :, yl, here, :] + (from_y[0, k] + from_y[1, k] + from_y[2, k])
        for d in range(1, 4):
            out_y.append(send(sum_y.at[:, lax.rem(x + d, 4)], next_y.at[d - 1], along_x(d)))
        return out_x, out_y

    def third_phase(size, out_x, out_y, sum_x, sum_y, next_x, next_y, both, arrived):
        view = sum_x.reshape(8, 2, 2, size, 128)
        for c in out_x:
            c.wait_recv()
        for k in range(8):
            both[k, 0:size, :] = view[k, yh, yl] + (next_x[0, k] + next_x[1, k] + next_x[2, k])
        for c in out_y:
            c.wait_recv()
        for k in range(8):
            both[k, size : 2 * size, :] = sum_y[k, x] + (next_y[0, k] + next_y[1, k] + next_y[2, k])
        return [send(both.at[lax.rem(z + d, 8)], arrived.at[d - 1], along_z(d)) for d in range(1, 8)]

    big_out_x, big_out_y = second_phase(0, 16, big_x, big_y, rx, ry, sx, sy, rx2, ry2)
    for c in copies_z:
        c.wait_recv()
    total = gz[z, :, 48:56, :]
    for d in range(7):
        total = total + rz[d]
    sz[...] = total.reshape(2, 4, 2, 8, 128)
    next_z = []
    for d in range(1, 4):
        next_z.append(send(sz.at[:, lax.rem(x + d, 4)], rz2.at[d - 1], along_x(d)))
    small_out_x, small_out_y = second_phase(16, 8, small_x, small_y, rxs, rys, sxs, syt, rx2s, ry2s)

    last_big = third_phase(16, big_out_x, big_out_y, sx, sy, rx2, ry2, sxy, rxy3)

    halo_finish(sp, 1, halo_two)

    def finish_two(c, bx, by, mid, rate):
        here = pl.ds(pl.multiple_of(by * 8 + 8, 8), 8)
        start = vp[c, pl.ds(bx * 8 + 1, 8), here, :]
        vnext[c, pl.ds(bx * 8, 8), pl.ds(pl.multiple_of(by * 8, 8), 8), :] = 0.75 * start + 0.25 * (
            mid + TIME_STEP * rate
        )

    section(sp, finish_two)

    for c in next_z:
        c.wait_recv()
    sz2[...] = sz[:, x] + (rz2[0] + rz2[1] + rz2[2])
    last_z = []
    for d in range(1, 4):
        k = lax.rem(y + d, 4)
        last_z.append(send(sz2.at[k // 2, k % 2], rz3.at[d - 1], along_y(d)))
    last_small = third_phase(8, small_out_x, small_out_y, sxs, syt, rx2s, ry2s, sxys, rxy3s)
    for c in last_big + last_z + last_small:
        c.wait_recv()
    front = sxy[z]
    tail = sxys[z]
    for d in range(7):
        front = front + rxy3[d]
        tail = tail + rxy3s[d]
    back = sz2[yh, yl] + (rz3[0] + rz3[1] + rz3[2])
    g = jnp.concatenate([front[:16], tail[:8], front[16:], tail[8:], back], axis=0)
    moment = BETA_ONE * mom1[...] + (1.0 - BETA_ONE) * g
    second = BETA_TWO * mom2[...] + (1.0 - BETA_TWO) * g * g
    corrected = moment / (1.0 - BETA_ONE**ADAM_STEP)
    direction[...] = corrected / (jnp.sqrt(second / (1.0 - BETA_TWO**ADAM_STEP)) + EPSILON)

    for c in (
        hist_copies + [pair_info, pair_y, pair_x, pair_w] + halo_one + halo_two
        + big_x + big_y + small_x + small_y + copies_z + big_out_x + big_out_y + small_out_x + small_out_y
        + next_z + last_big + last_small + last_z
    ):
        c.wait_send()


def local(velocity, target_field, w_in, w_mid, w_out, moment_one, moment_two, picks, owners, counts):
    any_space = pl.BlockSpec(memory_space=pl.ANY)
    vmem = pl.BlockSpec(memory_space=pltpu.VMEM)
    V = pltpu.VMEM
    next_velocity, direction = pl.pallas_call(
        kernel,
        out_shape=(
            pltpu.VMEM(velocity.shape, F32),
            pltpu.VMEM((56, 128), F32),
        ),
        in_specs=[any_space] * 5 + [vmem] * 5,
        out_specs=(vmem, vmem),
        scratch_shapes=[
            V((3, 26, 40, 128), F32),
            V((3, 26, 40, 128), F32),
            V((3, 24, 24, 128), F32),
            V((1536, 512), BF16),
            V((512, 512), BF16),
            V((512, 1536), BF16),
            V((1536, 512), BF16),
            V((1536, 512), BF16),
            V((256, 256), BF16),
            V((1152, 128), F32),
            V((1152, 128), F32),
            V((2, ROWS, WIDE), F32),
            V((2, ROWS, WIDE), BF16),
            V((2, ROWS, WIDE), F32),
            V((2, 32, 128), F32),
            V((2, 32, 128), F32),
            V((8, 128), F32),
            V((16, 8, 128), F32),
            V((2, 2, 3, 24, 128), F32),
            V((2, 2, 3, 24, 128), F32),
            V((512, WIDE), BF16),
            V((512, 512), F32),
            V((512, 512), F32),
            V((512, 512), BF16),
            V((512, 512), BF16),
            V((512, WIDE), BF16),
            V((512, 512), BF16),
            V((512, 512), BF16),
            V((7168, 128), F32),
            V((3, 16, 2, 16, 128), F32),
            V((3, 8, 4, 16, 128), F32),
            V((7, 16, 8, 128), F32),
            V((16, 2, 16, 128), F32),
            V((8, 4, 16, 128), F32),
            V((2, 4, 2, 8, 128), F32),
            V((3, 8, 16, 128), F32),
            V((3, 8, 16, 128), F32),
            V((3, 2, 2, 8, 128), F32),
            V((8, 32, 128), F32),
            V((2, 2, 8, 128), F32),
            V((7, 32, 128), F32),
            V((3, 8, 128), F32),
            V((3, 16, 2, 8, 128), F32),
            V((3, 8, 4, 8, 128), F32),
            V((16, 2, 8, 128), F32),
            V((8, 4, 8, 128), F32),
            V((3, 8, 8, 128), F32),
            V((3, 8, 8, 128), F32),
            V((8, 16, 128), F32),
            V((7, 16, 128), F32),
            pltpu.SemaphoreType.DMA((5,)),
            pltpu.SemaphoreType.DMA((80,)),
            pltpu.SemaphoreType.DMA((80,)),
        ],
        compiler_params=pltpu.CompilerParams(
            collective_id=0, has_side_effects=True, vmem_limit_bytes=60 * 2**20
        ),
    )(
        velocity, target_field, w_in, w_mid, w_out,
        moment_one.reshape(56, 128), moment_two.reshape(56, 128),
        picks.reshape(1, 32), owners.reshape(1, 32), counts,
    )
    return next_velocity, direction.reshape(7168)


def solution(mesh):
    return jax.shard_map(
        local,
        mesh=mesh,
        in_specs=(
            P(None, "gx", ("role", "gy"), None),
            P(None, "gx", ("role", "gy"), None),
            P(),
            P(),
            P(),
            P(("role", "gx", "gy")),
            P(("role", "gx", "gy")),
            P(("role", "gx", "gy")),
            P(("role", "gx", "gy")),
            P(("role", "gy"), "gx"),
        ),
        out_specs=(P(None, "gx", ("role", "gy"), None), P(("role", "gx", "gy"))),
        check_vma=False,
    )
```

```python
import math

import jax
import jax.numpy as jnp
from jax import lax
from jax.experimental import pallas as pl
from jax.experimental.pallas import tpu as pltpu
from jax.sharding import PartitionSpec as P

ADAM_STEP = 10
TIME_STEP = 0.2
VISCOSITY = 0.05
BETA_ONE = 0.9
BETA_TWO = 0.999
EPSILON = 1e-08
MESH = pl.DeviceIdType.MESH
F32 = jnp.float32
BF16 = jnp.bfloat16
NN = (((1,), (0,)), ((), ()))
NT = (((1,), (1,)), ((), ()))
TN = (((0,), (0,)), ((), ()))
GELU_K = math.sqrt(2.0 / math.pi)
GELU_C = 0.044715
ROWS = 144
WIDE = 1536


def dot(a, b, dims=NN):
    return lax.dot_general(a, b, dims, preferred_element_type=F32)


def gelu(a):
    t = jnp.tanh(GELU_K * (a + GELU_C * (a * a * a)))
    return a * (0.5 * (1.0 + t))


def gelu_and_slope(a):
    a2 = a * a
    t = jnp.tanh(GELU_K * (a + GELU_C * (a2 * a)))
    cdf = 0.5 * (1.0 + t)
    slope = cdf + (0.5 * GELU_K) * a * (1.0 - t * t) * (1.0 + (3.0 * GELU_C) * a2)
    return a * cdf, slope


def place(r, z, yh, x, yl):
    return {"role": r, "gx": z * 2 + yh, "gy": x * 2 + yl}


def kernel(
    vel_hbm, tgt_hbm, win_hbm, wmid_hbm, wout_hbm, mom1, mom2, picks, owners, counts,
    vnext, direction,
    vp, sp, tgt, w_in, w_mid, w_out, w_first, w_last, perm,
    t_zero, t_one, xf, xb, yf, info, weight, hist_out, hist, ysend, yrecv,
    xs, slope_one, slope_two, h_one, h_two, e_all, b_two, b_one,
    grad, rx, ry, rz, sx, sy, sz, rx2, ry2, rz2, sxy, sz2, rxy3, rz3,
    rxs, rys, sxs, syt, rx2s, ry2s, sxys, rxy3s, fx, fy, fxs, fys,
    load_sem, send_sem, recv_sem,
):
    r = lax.axis_index("role")
    i = lax.axis_index("gx")
    j = lax.axis_index("gy")
    z, yh, x, yl = i // 2, i % 2, j // 2, j % 2
    y = yh * 2 + yl
    q = r * 8 + j

    def at_q(k):
        k = lax.rem(k + 16, 16)
        return {"role": k // 8, "gx": i, "gy": k % 8}

    def at_i(k):
        return {"role": r, "gx": lax.rem(k + 16, 16), "gy": j}

    def along_x(d):
        return place(r, z, yh, lax.rem(x + d, 4), yl)

    def along_y(d):
        k = lax.rem(y + d, 4)
        return place(r, z, k // 2, x, k % 2)

    def along_z(d):
        return place(r, lax.rem(z + d, 8), yh, x, yl)

    pair = {"role": 1 - r, "gx": i, "gy": j}

    loads = []

    def load(src, dst):
        c = pltpu.make_async_copy(src, dst, load_sem.at[len(loads)])
        c.start()
        loads.append(c)
        return c

    load_v = load(vel_hbm, vp.at[:, 1:25, 8:32, :])
    load_t = load(tgt_hbm, tgt)
    load_wi = load(win_hbm, w_in)
    load_wo = load(wout_hbm, w_out)
    load_wm = load(wmid_hbm, w_mid)

    barrier = pltpu.get_barrier_semaphore()
    other = at_q(q + 2 * yl - 1)
    for d in (8, 7, 9, 6, 10, 5, 11, 4, 12, 3, 13, 2, 14, 1, 15):
        pl.semaphore_signal(barrier, inc=1, device_id=at_i(i + d), device_id_type=MESH)
    for d in range(1, 4):
        pl.semaphore_signal(barrier, inc=1, device_id=along_x(d), device_id_type=MESH)
    for who in (place(r, z, yh, x, 1 - yl), place(r, z, 1 - yh, x, 1 - yl), pair, other):
        pl.semaphore_signal(barrier, inc=1, device_id=who, device_id_type=MESH)

    def column(row):
        a = lax.broadcasted_iota(jnp.int32, (32, 32), 0)
        b = lax.broadcasted_iota(jnp.int32, (32, 32), 1)
        picked = jnp.where(a == b, jnp.broadcast_to(row, (32, 32)), 0.0)
        return jnp.broadcast_to(jnp.sum(picked, axis=1, keepdims=True), (32, 128))

    o = picks[...]
    one, nil = jnp.ones_like(o), jnp.zeros_like(o)
    over30 = jnp.where(o >= 30, one, nil)
    over15 = jnp.where(o >= 15, one, nil) + over30 + jnp.where(o >= 45, one, nil)
    first_block = (over30 * 3 + (over15 - 2 * over30)) * 16 + (o - 15 * over15)
    info[0] = column(first_block.astype(F32))
    owner = column(owners[...].astype(F32))
    slot = lax.broadcasted_iota(jnp.int32, (32, 128), 0)
    lane = lax.broadcasted_iota(jnp.int32, (32, 128), 1).astype(F32)
    alive = slot < jnp.broadcast_to(counts[...], (32, 128))
    match = jnp.where(alive, jnp.where(lane == owner, 1.0, 0.0), 0.0)
    hist_out[...] = jnp.broadcast_to(jnp.sum(match, axis=0, keepdims=True), (8, 128))
    hist[pl.ds(i, 1)] = hist_out[...].reshape(1, 8, 128)

    count = [0]

    def send(src, dst, who):
        k = count[0]
        count[0] += 1
        c = pltpu.make_async_remote_copy(
            src_ref=src, dst_ref=dst, send_sem=send_sem.at[k], recv_sem=recv_sem.at[k],
            device_id=who, device_id_type=MESH,
        )
        c.start()
        return c

    def halo_start(field, slot):
        flat = field.reshape(3 * 26 * 40, 128)
        for c in range(3):
            ysend[slot, 0, c] = flat[pl.ds((c * 26 + 1) * 40 + 8, 24, stride=40), :]
            ysend[slot, 1, c] = flat[pl.ds((c * 26 + 1) * 40 + 31, 24, stride=40), :]
        return [
            send(field.at[:, 1, 8:32, :], field.at[:, 25, 8:32, :], at_i(i - 1)),
            send(field.at[:, 24, 8:32, :], field.at[:, 0, 8:32, :], at_i(i + 1)),
            send(ysend.at[slot, 0], yrecv.at[slot, 1], at_q(q - 1)),
            send(ysend.at[slot, 1], yrecv.at[slot, 0], at_q(q + 1)),
        ]

    def halo_finish(field, slot, copies):
        for c in copies:
            c.wait_recv()
        flat = field.reshape(3 * 26 * 40, 128)
        for c in range(3):
            flat[pl.ds((c * 26 + 1) * 40 + 7, 24, stride=40), :] = yrecv[slot, 0, c]
            flat[pl.ds((c * 26 + 1) * 40 + 32, 24, stride=40), :] = yrecv[slot, 1, c]

    def turn(take):
        def body(k, carry):
            d = take(k // 3, k % 3).reshape(192, 128)
            rows = pl.ds(pl.multiple_of(k * 128, 128), 128)
            t_zero[rows, :] = d[:128].T
            t_one[rows, 0:64] = d[128:].T
            return carry

        lax.fori_loop(0, 9, body, 0)

    def take_from(field):
        def take(bx, by):
            return field[:, pl.ds(bx * 8 + 1, 8), pl.ds(pl.multiple_of(by * 8 + 8, 8), 8), :]

        return take

    half = lax.broadcasted_iota(jnp.int32, (ROWS, 128), 1)

    def rows_of(write):
        for oz in range(8):
            write(oz * 128, t_zero[pl.ds(oz, ROWS, stride=8), :])
        for k in range(4):
            a = t_one[pl.ds(2 * k, ROWS, stride=8), :]
            b = t_one[pl.ds(2 * k + 1, ROWS, stride=8), :]
            write(1024 + k * 128, jnp.where(half < 64, a, pltpu.roll(b, 64, 1)))

    pr = lax.broadcasted_iota(jnp.int32, (256, 256), 0)
    pc = lax.broadcasted_iota(jnp.int32, (256, 256), 1)
    perm[...] = jnp.where(pc == (pr & 31) * 8 + (pr >> 5), 1.0, 0.0).astype(BF16)

    pl.semaphore_wait(barrier, 22)
    hist_copies = [send(hist_out, hist.at[i], at_i(i + d)) for d in (8, 7, 9, 6, 10, 5, 11, 4, 12, 3, 13, 2, 14, 1, 15)]
    pair_info = send(info.at[0], info.at[1], pair)

    load_v.wait()
    turn(take_from(vp))

    def write_x(at, tile):
        xf[0, :, at : at + 128] = tile
        xb[0, :, at : at + 128] = tile.astype(BF16)

    rows_of(write_x)

    pair_x = send(xf.at[0], xf.at[1], pair)
    halo_one = halo_start(vp, 0)

    load_t.wait()

    def take_target(bx, by):
        return tgt[:, pl.ds(bx * 8, 8), pl.ds(pl.multiple_of(by * 8, 8), 8), :]

    turn(take_target)
    for g in range(6):
        tiles = []
        src, base = (t_zero, g) if g < 4 else (t_one, g - 4)
        for quad in range(2):
            tile = None
            for m in range(4):
                part = src[pl.ds(4 * quad + m, ROWS, stride=8), :]
                shift = (32 * (m - base)) % 128
                if shift:
                    part = pltpu.roll(part, shift, 1)
                tile = part if tile is None else jnp.where(half >= 32 * m, part, tile)
            tiles.append(tile.astype(BF16))
        yf[0, :, 256 * g : 256 * g + 256] = dot(jnp.concatenate(tiles, axis=1), perm[...])
    pair_y = send(yf.at[0], yf.at[1], pair)

    def block_order(g, value, dst):
        for oz in range(8):
            at = oz * 128 + 32 * g if g < 4 else 1024 + oz * 64 + 32 * (g - 4)
            dst[at : at + 32, :] = value[32 * oz : 32 * oz + 32].astype(BF16)

    load_wi.wait()
    for g in range(6):
        block_order(g, dot(perm[...], w_in[256 * g : 256 * g + 256, :]), w_first)

    def choose(s):
        start = info[s]
        start = jnp.concatenate([start, start], axis=1)[:, :ROWS]
        block = lax.broadcasted_iota(jnp.int32, (32, ROWS), 1).astype(F32)
        return jnp.concatenate(
            [
                jnp.where(block == start + float(k // 4 * 48 + k // 2 % 2 * 16 + k % 2), 1.0, 0.0)
                for k in range(8)
            ],
            axis=0,
        ).astype(BF16)

    def forward(s):
        rows = slice(256 * s, 256 * s + 256)
        chosen = choose(s)
        for n in range(3):
            cols = slice(512 * n, 512 * n + 512)
            xs[rows, cols] = dot(chosen, xb[s, :, cols]).astype(BF16)
        a, slope = gelu_and_slope(dot(xs[rows, :], w_first[...]))
        slope_one[rows, :] = slope
        h1 = a.astype(BF16)
        h_one[rows, :] = h1
        a, slope = gelu_and_slope(dot(h1, w_mid[...]))
        slope_two[rows, :] = slope
        h_two[rows, :] = a.astype(BF16)

    def backward(s):
        rows = slice(256 * s, 256 * s + 256)
        chosen = choose(s)
        w8 = 2.0 * jnp.concatenate([weight[s]] * 8, axis=0)
        w8 = jnp.concatenate([w8] * 4, axis=1)
        up = None
        for n in range(3):
            cols = slice(512 * n, 512 * n + 512)
            target = dot(chosen, yf[s, :, cols].astype(BF16))
            e = (w8 * (dot(h_two[rows, :], w_out[:, cols]) - target)).astype(BF16)
            e_all[rows, cols] = e
            part = dot(e, w_out[:, cols], NT)
            up = part if up is None else up + part
        b_two[rows, :] = (slope_two[rows, :] * up).astype(BF16)

    def closure(rows):
        q1 = gelu(dot(rows, w_first[...])).astype(BF16)
        q2 = gelu(dot(q1, w_mid[...])).astype(BF16)
        for n in range(2):
            out = dot(q2, w_last[512 * n : 512 * n + 512, :], NT)
            for m in range(4):
                t_zero[pl.ds(4 * n + m, ROWS, stride=8), :] = out[:, 128 * m : 128 * m + 128]
        out = dot(q2, w_last[1024:1536, :], NT)
        for m in range(4):
            tile = out[:, 128 * m : 128 * m + 128]
            t_one[pl.ds(2 * m, ROWS, stride=8), :] = tile
            t_one[pl.ds(2 * m + 1, ROWS, stride=8), :] = pltpu.roll(tile, 64, 1)

    def section(field, finish):
        def body(k, carry):
            bx, by = k // 3, k % 3
            rows = pl.ds(pl.multiple_of(k * 128, 128), 128)
            closed = [None, None, None]
            front = t_zero[rows, :].T
            closed[0] = front[:64].reshape(8, 8, 128)
            closed[1] = front[64:].reshape(8, 8, 128)
            closed[2] = t_one[rows, :].T[:64].reshape(8, 8, 128)
            here = pl.ds(pl.multiple_of(by * 8 + 8, 8), 8)
            around = pl.ds(pl.multiple_of(by * 8, 8), 24)
            center = [field[c, pl.ds(bx * 8 + 1, 8), here, :] for c in range(3)]
            for c in range(3):
                mid = center[c]
                first_up = field[c, pl.ds(bx * 8 + 2, 8), here, :]
                first_down = field[c, pl.ds(bx * 8, 8), here, :]
                window = field[c, pl.ds(bx * 8 + 1, 8), around, :]
                second_up = window[:, 9:17, :]
                second_down = window[:, 7:15, :]
                third_up = pltpu.roll(mid, 127, 2)
                third_down = pltpu.roll(mid, 1, 2)
                advect = (
                    center[0] * ((first_up - first_down) * 0.5)
                    + center[1] * ((second_up - second_down) * 0.5)
                    + center[2] * ((third_up - third_down) * 0.5)
                )
                spread = (
                    first_up + first_down + (second_up + second_down) + (third_up + third_down) - 6.0 * mid
                )
                finish(c, bx, by, mid, VISCOSITY * spread - advect + closed[c])
            return carry

        lax.fori_loop(0, 9, body, 0)

    load_wm.wait()
    load_wo.wait()
    forward(0)
    pair_info.wait_recv()
    pair_x.wait_recv()
    xb[1] = xf[1].astype(BF16)
    forward(1)

    for c in hist_copies:
        c.wait_recv()
    totals = jnp.sum(hist[...], axis=0)
    inverse = 1.0 / jnp.maximum(totals, 1.0)
    own_weight = jnp.sum(match * inverse[0:1, :], axis=1, keepdims=True)
    weight[0] = jnp.broadcast_to(own_weight, (32, 128))
    pair_w = send(weight.at[0], weight.at[1], pair)

    backward(0)
    pair_y.wait_recv()
    pair_w.wait_recv()
    backward(1)

    def put(value, start, stride, size):
        for cb in range(value.shape[1] // 128):
            grad_flat[pl.ds(start + cb, size, stride=stride), :] = value[:, cb * 128 : cb * 128 + 128]

    grad_flat = grad.reshape(7168, 128)

    @pl.when(r == 0)
    def _():
        for s in range(2):
            rows = slice(256 * s, 256 * s + 256)
            up = dot(b_two[rows, :], w_mid[...], NT)
            b_one[rows, :] = (slope_one[rows, :] * up).astype(BF16)
        for k in range(4):
            part = dot(xs[:, 256 * k : 256 * k + 256], b_one[...], TN)
            put(part[:128], 8 * k, 32, 128)
            put(part[128:], 8 * k + 4, 32, 128)
        for k in range(2):
            part = dot(xs[:, 1024 + 256 * k : 1280 + 256 * k], b_one[...], TN)
            for m in range(4):
                put(part[64 * m : 64 * m + 64], 4096 + 4 * (4 * k + m), 32, 64)
        put(dot(h_one[:, 0:256], b_two[...], TN), 6144, 4, 256)

    @pl.when(r == 1)
    def _():
        for k in range(2):
            for n in range(3):
                part = dot(h_two[:, 256 * k : 256 * k + 256], e_all[:, 512 * n : 512 * n + 512], TN)
                put(part, 1024 + 3072 * k + 4 * n, 12, 256)
        put(dot(h_one[:, 256:512], b_two[...], TN), 0, 4, 256)

    gx5 = grad.reshape(16, 4, 2, 56, 128)
    gy6 = grad.reshape(8, 2, 4, 2, 56, 128)
    gz = grad.reshape(8, 16, 56, 128)
    copies_z = []

    up_x, low_x, up_y, low_y = lax.rem(x + 1, 4), lax.rem(x + 3, 4), lax.rem(y + 1, 4), lax.rem(y + 3, 4)

    def for_x(to, part, rows):
        return gx5.at[8 * part : 8 * part + 8, to, :, rows, :]

    def for_y(to, part, rows):
        return gy6.at[4 * part : 4 * part + 4, to // 2, :, to % 2, rows, :]

    def far_phase(at, size, far_x, far_y):
        rx_rows, ry_rows = slice(at, at + size), slice(24 + at, 24 + at + size)
        two_x, two_y = lax.rem(x + 2, 4), lax.rem(y + 2, 4)
        return (
            [
                send(for_x(two_x, 0, rx_rows), far_x.at[0], along_x(1)),
                send(for_x(two_x, 1, rx_rows), far_x.at[1], along_x(3)),
            ],
            [
                send(for_y(two_y, 0, ry_rows), far_y.at[0], along_y(1)),
                send(for_y(two_y, 1, ry_rows), far_y.at[1], along_y(3)),
            ],
        )

    def near_phase(at, size, from_x, from_y):
        rx_rows, ry_rows = slice(at, at + size), slice(24 + at, 24 + at + size)
        return (
            [
                send(for_x(up_x, 1, rx_rows), from_x.at[0, 1], along_x(1)),
                send(for_x(low_x, 0, rx_rows), from_x.at[1, 0], along_x(3)),
            ],
            [
                send(for_y(up_y, 1, ry_rows), from_y.at[0, 1], along_y(1)),
                send(for_y(low_y, 0, ry_rows), from_y.at[1, 0], along_y(3)),
            ],
        )

    def merge(at, size, far, near, far_x, far_y, from_x, from_y):
        rx_rows, ry_rows = slice(at, at + size), slice(24 + at, 24 + at + size)
        for part, to, way in ((0, up_x, 1), (1, low_x, 3)):
            far[0][part].wait_recv()
            for k in range(8):
                gx5[8 * part + k, to, :, rx_rows, :] = gx5[8 * part + k, to, :, rx_rows, :] + far_x[part, k]
            near[0].append(send(for_x(to, part, rx_rows), from_x.at[part, part], along_x(way)))
        for part, to, way in ((0, up_y, 1), (1, low_y, 3)):
            far[1][part].wait_recv()
            for k in range(4):
                there = (4 * part + k, to // 2, slice(None), to % 2, ry_rows, slice(None))
                gy6[there] = gy6[there] + far_y[part, k]
            near[1].append(send(for_y(to, part, ry_rows), from_y.at[part, part], along_y(way)))

    big_far = far_phase(0, 16, fx, fy)
    big_near = near_phase(0, 16, rx, ry)
    small_far = far_phase(16, 8, fxs, fys)
    for d in (4, 3, 5, 2, 6, 1, 7):
        copies_z.append(send(gz.at[lax.rem(z + d, 8), :, 48:56, :], rz.at[d - 1], along_z(d)))
    merge(0, 16, big_far, big_near, fx, fy, rx, ry)
    small_near = near_phase(16, 8, rxs, rys)

    for g in range(6):
        block_order(g, dot(perm[...], w_out[:, 256 * g : 256 * g + 256], NT), w_last)
    closure(xb[0])
    merge(16, 8, small_far, small_near, fxs, fys, rxs, rys)
    halo_finish(vp, 0, halo_one)

    def finish_one(c, bx, by, mid, rate):
        here = pl.ds(pl.multiple_of(by * 8 + 8, 8), 8)
        sp[c, pl.ds(bx * 8 + 1, 8), here, :] = mid + TIME_STEP * rate

    section(vp, finish_one)
    halo_two = halo_start(sp, 1)
    turn(take_from(sp))

    def write_second(at, tile):
        xb[1, :, at : at + 128] = tile.astype(BF16)

    rows_of(write_second)
    closure(xb[1])
    def second_phase(at, size, to_x, to_y, from_x, from_y, sum_x, sum_y, next_x, next_y):
        out_x, out_y = [], []
        for c in to_x:
            c.wait_recv()
        for k in range(16):
            sum_x[k] = gx5[k, x, :, at : at + size, :] + (from_x[0, k // 8, k % 8] + from_x[1, k // 8, k % 8])
        view = sum_x.reshape(8, 2, 2, size, 128)
        for d in range(1, 4):
            k = lax.rem(y + d, 4)
            out_x.append(send(view.at[:, k // 2, k % 2], next_x.at[d - 1], along_y(d)))
        for c in to_y:
            c.wait_recv()
        here = slice(24 + at, 24 + at + size)
        for k in range(8):
            sum_y[k] = gy6[k, yh, :, yl, here, :] + (from_y[0, k // 4, k % 4] + from_y[1, k // 4, k % 4])
        for d in range(1, 4):
            out_y.append(send(sum_y.at[:, lax.rem(x + d, 4)], next_y.at[d - 1], along_x(d)))
        return out_x, out_y

    def third_phase(size, out_x, out_y, sum_x, sum_y, next_x, next_y, both, arrived):
        view = sum_x.reshape(8, 2, 2, size, 128)
        for c in out_x:
            c.wait_recv()
        for k in range(8):
            both[k, 0:size, :] = view[k, yh, yl] + (next_x[0, k] + next_x[1, k] + next_x[2, k])
        for c in out_y:
            c.wait_recv()
        for k in range(8):
            both[k, size : 2 * size, :] = sum_y[k, x] + (next_y[0, k] + next_y[1, k] + next_y[2, k])
        return [send(both.at[lax.rem(z + d, 8)], arrived.at[d - 1], along_z(d)) for d in (4, 3, 5, 2, 6, 1, 7)]

    big_out_x, big_out_y = second_phase(0, 16, big_near[0], big_near[1], rx, ry, sx, sy, rx2, ry2)
    for c in copies_z:
        c.wait_recv()
    total = gz[z, :, 48:56, :]
    for d in range(7):
        total = total + rz[d]
    sz[...] = total.reshape(2, 4, 2, 8, 128)
    next_z = []
    for d in range(1, 4):
        next_z.append(send(sz.at[:, lax.rem(x + d, 4)], rz2.at[d - 1], along_x(d)))
    small_out_x, small_out_y = second_phase(16, 8, small_near[0], small_near[1], rxs, rys, sxs, syt, rx2s, ry2s)

    last_big = third_phase(16, big_out_x, big_out_y, sx, sy, rx2, ry2, sxy, rxy3)

    halo_finish(sp, 1, halo_two)

    def finish_two(c, bx, by, mid, rate):
        here = pl.ds(pl.multiple_of(by * 8 + 8, 8), 8)
        start = vp[c, pl.ds(bx * 8 + 1, 8), here, :]
        vnext[c, pl.ds(bx * 8, 8), pl.ds(pl.multiple_of(by * 8, 8), 8), :] = 0.75 * start + 0.25 * (
            mid + TIME_STEP * rate
        )

    section(sp, finish_two)

    for c in next_z:
        c.wait_recv()
    sz2[...] = sz[:, x] + (rz2[0] + rz2[1] + rz2[2])
    last_z = []
    for d in range(1, 4):
        k = lax.rem(y + d, 4)
        last_z.append(send(sz2.at[k // 2, k % 2], rz3.at[d - 1], along_y(d)))
    last_small = third_phase(8, small_out_x, small_out_y, sxs, syt, rx2s, ry2s, sxys, rxy3s)
    for c in last_big + last_z + last_small:
        c.wait_recv()
    front = sxy[z]
    tail = sxys[z]
    for d in range(7):
        front = front + rxy3[d]
        tail = tail + rxy3s[d]
    back = sz2[yh, yl] + (rz3[0] + rz3[1] + rz3[2])
    g = jnp.concatenate([front[:16], tail[:8], front[16:], tail[8:], back], axis=0)
    moment = BETA_ONE * mom1[...] + (1.0 - BETA_ONE) * g
    second = BETA_TWO * mom2[...] + (1.0 - BETA_TWO) * g * g
    corrected = moment / (1.0 - BETA_ONE**ADAM_STEP)
    direction[...] = corrected / (jnp.sqrt(second / (1.0 - BETA_TWO**ADAM_STEP)) + EPSILON)

    for c in (
        hist_copies + [pair_info, pair_y, pair_x, pair_w] + halo_one + halo_two
        + big_far[0] + big_far[1] + big_near[0] + big_near[1] + small_far[0] + small_far[1]
        + small_near[0] + small_near[1] + copies_z + big_out_x + big_out_y + small_out_x + small_out_y
        + next_z + last_big + last_small + last_z
    ):
        c.wait_send()


def local(velocity, target_field, w_in, w_mid, w_out, moment_one, moment_two, picks, owners, counts):
    any_space = pl.BlockSpec(memory_space=pl.ANY)
    vmem = pl.BlockSpec(memory_space=pltpu.VMEM)
    V = pltpu.VMEM
    next_velocity, direction = pl.pallas_call(
        kernel,
        out_shape=(
            pltpu.VMEM(velocity.shape, F32),
            pltpu.VMEM((56, 128), F32),
        ),
        in_specs=[any_space] * 5 + [vmem] * 5,
        out_specs=(vmem, vmem),
        scratch_shapes=[
            V((3, 26, 40, 128), F32),
            V((3, 26, 40, 128), F32),
            V((3, 24, 24, 128), F32),
            V((1536, 512), BF16),
            V((512, 512), BF16),
            V((512, 1536), BF16),
            V((1536, 512), BF16),
            V((1536, 512), BF16),
            V((256, 256), BF16),
            V((1152, 128), F32),
            V((1152, 128), F32),
            V((2, ROWS, WIDE), F32),
            V((2, ROWS, WIDE), BF16),
            V((2, ROWS, WIDE), F32),
            V((2, 32, 128), F32),
            V((2, 32, 128), F32),
            V((8, 128), F32),
            V((16, 8, 128), F32),
            V((2, 2, 3, 24, 128), F32),
            V((2, 2, 3, 24, 128), F32),
            V((512, WIDE), BF16),
            V((512, 512), F32),
            V((512, 512), F32),
            V((512, 512), BF16),
            V((512, 512), BF16),
            V((512, WIDE), BF16),
            V((512, 512), BF16),
            V((512, 512), BF16),
            V((7168, 128), F32),
            V((2, 2, 8, 2, 16, 128), F32),
            V((2, 2, 4, 4, 16, 128), F32),
            V((7, 16, 8, 128), F32),
            V((16, 2, 16, 128), F32),
            V((8, 4, 16, 128), F32),
            V((2, 4, 2, 8, 128), F32),
            V((3, 8, 16, 128), F32),
            V((3, 8, 16, 128), F32),
            V((3, 2, 2, 8, 128), F32),
            V((8, 32, 128), F32),
            V((2, 2, 8, 128), F32),
            V((7, 32, 128), F32),
            V((3, 8, 128), F32),
            V((2, 2, 8, 2, 8, 128), F32),
            V((2, 2, 4, 4, 8, 128), F32),
            V((16, 2, 8, 128), F32),
            V((8, 4, 8, 128), F32),
            V((3, 8, 8, 128), F32),
            V((3, 8, 8, 128), F32),
            V((8, 16, 128), F32),
            V((7, 16, 128), F32),
            V((2, 8, 2, 16, 128), F32),
            V((2, 4, 4, 16, 128), F32),
            V((2, 8, 2, 8, 128), F32),
            V((2, 4, 4, 8, 128), F32),
            pltpu.SemaphoreType.DMA((5,)),
            pltpu.SemaphoreType.DMA((90,)),
            pltpu.SemaphoreType.DMA((90,)),
        ],
        compiler_params=pltpu.CompilerParams(
            collective_id=0, has_side_effects=True, vmem_limit_bytes=60 * 2**20
        ),
    )(
        velocity, target_field, w_in, w_mid, w_out,
        moment_one.reshape(56, 128), moment_two.reshape(56, 128),
        picks.reshape(1, 32), owners.reshape(1, 32), counts,
    )
    return next_velocity, direction.reshape(7168)


def solution(mesh):
    return jax.shard_map(
        local,
        mesh=mesh,
        in_specs=(
            P(None, "gx", ("role", "gy"), None),
            P(None, "gx", ("role", "gy"), None),
            P(),
            P(),
            P(),
            P(("role", "gx", "gy")),
            P(("role", "gx", "gy")),
            P(("role", "gx", "gy")),
            P(("role", "gx", "gy")),
            P(("role", "gy"), "gx"),
        ),
        out_specs=(P(None, "gx", ("role", "gy"), None), P(("role", "gx", "gy"))),
        check_vma=False,
    )
```

```python
import math

import jax
import jax.numpy as jnp
from jax import lax
from jax.experimental import pallas as pl
from jax.experimental.pallas import tpu as pltpu
from jax.sharding import PartitionSpec as P

ADAM_STEP = 10
TIME_STEP = 0.2
VISCOSITY = 0.05
BETA_ONE = 0.9
BETA_TWO = 0.999
EPSILON = 1e-08
MESH = pl.DeviceIdType.MESH
F32 = jnp.float32
BF16 = jnp.bfloat16
NN = (((1,), (0,)), ((), ()))
NT = (((1,), (1,)), ((), ()))
TN = (((0,), (0,)), ((), ()))
GELU_K = math.sqrt(2.0 / math.pi)
GELU_C = 0.044715
ROWS = 144
WIDE = 1536


def dot(a, b, dims=NN):
    return lax.dot_general(a, b, dims, preferred_element_type=F32)


def gelu(a):
    t = jnp.tanh(GELU_K * (a + GELU_C * (a * a * a)))
    return a * (0.5 * (1.0 + t))


def gelu_and_slope(a):
    a2 = a * a
    t = jnp.tanh(GELU_K * (a + GELU_C * (a2 * a)))
    cdf = 0.5 * (1.0 + t)
    slope = cdf + (0.5 * GELU_K) * a * (1.0 - t * t) * (1.0 + (3.0 * GELU_C) * a2)
    return a * cdf, slope


def place(r, z, yh, x, yl):
    return {"role": r, "gx": z * 2 + yh, "gy": x * 2 + yl}


def kernel(
    vel_hbm, tgt_hbm, win_hbm, wmid_hbm, wout_hbm, mom1, mom2, picks, owners, counts,
    vnext, direction,
    vp, sp, tgt, w_in, w_mid, w_out, w_first, w_last, perm,
    t_zero, t_one, xf, xb, yf, info, weight, hist_out, hist, ysend, yrecv,
    xs, slope_one, slope_two, h_one, h_two, e_all, b_two, b_one,
    grad, rx, ry, rz, sx, sy, sz, rx2, ry2, rz2, sxy, sz2, rxy3, rz3,
    rxs, rys, sxs, syt, rx2s, ry2s, sxys, rxy3s, fx, fy, fxs, fys,
    load_sem, send_sem, recv_sem,
):
    r = lax.axis_index("role")
    i = lax.axis_index("gx")
    j = lax.axis_index("gy")
    z, yh, x, yl = i // 2, i % 2, j // 2, j % 2
    y = yh * 2 + yl
    q = r * 8 + j

    def at_q(k):
        k = lax.rem(k + 16, 16)
        return {"role": k // 8, "gx": i, "gy": k % 8}

    def at_i(k):
        return {"role": r, "gx": lax.rem(k + 16, 16), "gy": j}

    def along_x(d):
        return place(r, z, yh, lax.rem(x + d, 4), yl)

    def along_y(d):
        k = lax.rem(y + d, 4)
        return place(r, z, k // 2, x, k % 2)

    def along_z(d):
        return place(r, lax.rem(z + d, 8), yh, x, yl)

    pair = {"role": 1 - r, "gx": i, "gy": j}

    loads = []

    def load(src, dst):
        c = pltpu.make_async_copy(src, dst, load_sem.at[len(loads)])
        c.start()
        loads.append(c)
        return c

    load_v = load(vel_hbm, vp.at[:, 1:25, 8:32, :])
    load_t = load(tgt_hbm, tgt)
    load_wi = load(win_hbm, w_in)
    load_wo = load(wout_hbm, w_out)
    load_wm = load(wmid_hbm, w_mid)

    barrier = pltpu.get_barrier_semaphore()
    other = at_q(q + 2 * yl - 1)
    for d in (8, 7, 9, 6, 10, 5, 11, 4, 12, 3, 13, 2, 14, 1, 15):
        pl.semaphore_signal(barrier, inc=1, device_id=at_i(i + d), device_id_type=MESH)
    for d in range(1, 4):
        pl.semaphore_signal(barrier, inc=1, device_id=along_x(d), device_id_type=MESH)
    for who in (place(r, z, yh, x, 1 - yl), place(r, z, 1 - yh, x, 1 - yl), pair, other):
        pl.semaphore_signal(barrier, inc=1, device_id=who, device_id_type=MESH)

    def column(row):
        a = lax.broadcasted_iota(jnp.int32, (32, 32), 0)
        b = lax.broadcasted_iota(jnp.int32, (32, 32), 1)
        picked = jnp.where(a == b, jnp.broadcast_to(row, (32, 32)), 0.0)
        return jnp.broadcast_to(jnp.sum(picked, axis=1, keepdims=True), (32, 128))

    o = picks[...]
    one, nil = jnp.ones_like(o), jnp.zeros_like(o)
    over30 = jnp.where(o >= 30, one, nil)
    over15 = jnp.where(o >= 15, one, nil) + over30 + jnp.where(o >= 45, one, nil)
    first_block = (over30 * 3 + (over15 - 2 * over30)) * 16 + (o - 15 * over15)
    info[0] = column(first_block.astype(F32))
    owner = column(owners[...].astype(F32))
    slot = lax.broadcasted_iota(jnp.int32, (32, 128), 0)
    lane = lax.broadcasted_iota(jnp.int32, (32, 128), 1).astype(F32)
    alive = slot < jnp.broadcast_to(counts[...], (32, 128))
    match = jnp.where(alive, jnp.where(lane == owner, 1.0, 0.0), 0.0)
    hist_out[...] = jnp.broadcast_to(jnp.sum(match, axis=0, keepdims=True), (8, 128))
    hist[pl.ds(i, 1)] = hist_out[...].reshape(1, 8, 128)

    count = [0]

    def send(src, dst, who):
        k = count[0]
        count[0] += 1
        c = pltpu.make_async_remote_copy(
            src_ref=src, dst_ref=dst, send_sem=send_sem.at[k], recv_sem=recv_sem.at[k],
            device_id=who, device_id_type=MESH,
        )
        c.start()
        return c

    def halo_start(field, slot):
        flat = field.reshape(3 * 26 * 40, 128)
        for c in range(3):
            ysend[slot, 0, c] = flat[pl.ds((c * 26 + 1) * 40 + 8, 24, stride=40), :]
            ysend[slot, 1, c] = flat[pl.ds((c * 26 + 1) * 40 + 31, 24, stride=40), :]
        return [
            send(field.at[:, 1, 8:32, :], field.at[:, 25, 8:32, :], at_i(i - 1)),
            send(field.at[:, 24, 8:32, :], field.at[:, 0, 8:32, :], at_i(i + 1)),
            send(ysend.at[slot, 0], yrecv.at[slot, 1], at_q(q - 1)),
            send(ysend.at[slot, 1], yrecv.at[slot, 0], at_q(q + 1)),
        ]

    def halo_finish(field, slot, copies):
        for c in copies:
            c.wait_recv()
        flat = field.reshape(3 * 26 * 40, 128)
        for c in range(3):
            flat[pl.ds((c * 26 + 1) * 40 + 7, 24, stride=40), :] = yrecv[slot, 0, c]
            flat[pl.ds((c * 26 + 1) * 40 + 32, 24, stride=40), :] = yrecv[slot, 1, c]

    def turn(take):
        def body(k, carry):
            d = take(k // 3, k % 3).reshape(192, 128)
            rows = pl.ds(pl.multiple_of(k * 128, 128), 128)
            t_zero[rows, :] = d[:128].T
            t_one[rows, 0:64] = d[128:].T
            return carry

        lax.fori_loop(0, 9, body, 0)

    def take_from(field):
        def take(bx, by):
            return field[:, pl.ds(bx * 8 + 1, 8), pl.ds(pl.multiple_of(by * 8 + 8, 8), 8), :]

        return take

    half = lax.broadcasted_iota(jnp.int32, (ROWS, 128), 1)

    def rows_of(write):
        for oz in range(8):
            write(oz * 128, t_zero[pl.ds(oz, ROWS, stride=8), :])
        for k in range(4):
            a = t_one[pl.ds(2 * k, ROWS, stride=8), :]
            b = t_one[pl.ds(2 * k + 1, ROWS, stride=8), :]
            write(1024 + k * 128, jnp.where(half < 64, a, pltpu.roll(b, 64, 1)))

    pr = lax.broadcasted_iota(jnp.int32, (256, 256), 0)
    pc = lax.broadcasted_iota(jnp.int32, (256, 256), 1)
    perm[...] = jnp.where(pc == (pr & 31) * 8 + (pr >> 5), 1.0, 0.0).astype(BF16)

    pl.semaphore_wait(barrier, 22)
    hist_copies = [send(hist_out, hist.at[i], at_i(i + d)) for d in (8, 7, 9, 6, 10, 5, 11, 4, 12, 3, 13, 2, 14, 1, 15)]
    pair_info = send(info.at[0], info.at[1], pair)

    load_v.wait()
    turn(take_from(vp))

    def write_x(at, tile):
        xf[0, :, at : at + 128] = tile
        xb[0, :, at : at + 128] = tile.astype(BF16)

    rows_of(write_x)

    pair_x = send(xf.at[0], xf.at[1], pair)
    halo_one = halo_start(vp, 0)

    load_t.wait()

    def take_target(bx, by):
        return tgt[:, pl.ds(bx * 8, 8), pl.ds(pl.multiple_of(by * 8, 8), 8), :]

    turn(take_target)
    for g in range(6):
        tiles = []
        src, base = (t_zero, g) if g < 4 else (t_one, g - 4)
        for quad in range(2):
            tile = None
            for m in range(4):
                part = src[pl.ds(4 * quad + m, ROWS, stride=8), :]
                shift = (32 * (m - base)) % 128
                if shift:
                    part = pltpu.roll(part, shift, 1)
                tile = part if tile is None else jnp.where(half >= 32 * m, part, tile)
            tiles.append(tile.astype(BF16))
        yf[0, :, 256 * g : 256 * g + 256] = dot(jnp.concatenate(tiles, axis=1), perm[...])
    pair_y = send(yf.at[0], yf.at[1], pair)

    def block_order(g, value, dst):
        for oz in range(8):
            at = oz * 128 + 32 * g if g < 4 else 1024 + oz * 64 + 32 * (g - 4)
            dst[at : at + 32, :] = value[32 * oz : 32 * oz + 32].astype(BF16)

    load_wi.wait()
    for g in range(6):
        block_order(g, dot(perm[...], w_in[256 * g : 256 * g + 256, :]), w_first)

    def choose(s):
        start = info[s]
        start = jnp.concatenate([start, start], axis=1)[:, :ROWS]
        block = lax.broadcasted_iota(jnp.int32, (32, ROWS), 1).astype(F32)
        return jnp.concatenate(
            [
                jnp.where(block == start + float(k // 4 * 48 + k // 2 % 2 * 16 + k % 2), 1.0, 0.0)
                for k in range(8)
            ],
            axis=0,
        ).astype(BF16)

    def forward(s):
        rows = slice(256 * s, 256 * s + 256)
        chosen = choose(s)
        for n in range(3):
            cols = slice(512 * n, 512 * n + 512)
            xs[rows, cols] = dot(chosen, xb[s, :, cols]).astype(BF16)
        a, slope = gelu_and_slope(dot(xs[rows, :], w_first[...]))
        slope_one[rows, :] = slope
        h1 = a.astype(BF16)
        h_one[rows, :] = h1
        a, slope = gelu_and_slope(dot(h1, w_mid[...]))
        slope_two[rows, :] = slope
        h_two[rows, :] = a.astype(BF16)

    def backward(s):
        rows = slice(256 * s, 256 * s + 256)
        chosen = choose(s)
        w8 = 2.0 * jnp.concatenate([weight[s]] * 8, axis=0)
        w8 = jnp.concatenate([w8] * 4, axis=1)
        up = None
        for n in range(3):
            cols = slice(512 * n, 512 * n + 512)
            target = dot(chosen, yf[s, :, cols].astype(BF16))
            e = (w8 * (dot(h_two[rows, :], w_out[:, cols]) - target)).astype(BF16)
            e_all[rows, cols] = e
            part = dot(e, w_out[:, cols], NT)
            up = part if up is None else up + part
        b_two[rows, :] = (slope_two[rows, :] * up).astype(BF16)

    def closure(rows):
        q1 = gelu(dot(rows, w_first[...])).astype(BF16)
        q2 = gelu(dot(q1, w_mid[...])).astype(BF16)
        for n in range(2):
            out = dot(q2, w_last[512 * n : 512 * n + 512, :], NT)
            for m in range(4):
                t_zero[pl.ds(4 * n + m, ROWS, stride=8), :] = out[:, 128 * m : 128 * m + 128]
        out = dot(q2, w_last[1024:1536, :], NT)
        for m in range(4):
            tile = out[:, 128 * m : 128 * m + 128]
            t_one[pl.ds(2 * m, ROWS, stride=8), :] = tile
            t_one[pl.ds(2 * m + 1, ROWS, stride=8), :] = pltpu.roll(tile, 64, 1)

    def section(field, finish):
        def body(k, carry):
            bx, by = k // 3, k % 3
            rows = pl.ds(pl.multiple_of(k * 128, 128), 128)
            closed = [None, None, None]
            front = t_zero[rows, :].T
            closed[0] = front[:64].reshape(8, 8, 128)
            closed[1] = front[64:].reshape(8, 8, 128)
            closed[2] = t_one[rows, :].T[:64].reshape(8, 8, 128)
            here = pl.ds(pl.multiple_of(by * 8 + 8, 8), 8)
            around = pl.ds(pl.multiple_of(by * 8, 8), 24)
            center = [field[c, pl.ds(bx * 8 + 1, 8), here, :] for c in range(3)]
            for c in range(3):
                mid = center[c]
                first_up = field[c, pl.ds(bx * 8 + 2, 8), here, :]
                first_down = field[c, pl.ds(bx * 8, 8), here, :]
                window = field[c, pl.ds(bx * 8 + 1, 8), around, :]
                second_up = window[:, 9:17, :]
                second_down = window[:, 7:15, :]
                third_up = pltpu.roll(mid, 127, 2)
                third_down = pltpu.roll(mid, 1, 2)
                advect = (
                    center[0] * ((first_up - first_down) * 0.5)
                    + center[1] * ((second_up - second_down) * 0.5)
                    + center[2] * ((third_up - third_down) * 0.5)
                )
                spread = (
                    first_up + first_down + (second_up + second_down) + (third_up + third_down) - 6.0 * mid
                )
                finish(c, bx, by, mid, VISCOSITY * spread - advect + closed[c])
            return carry

        lax.fori_loop(0, 9, body, 0)

    load_wm.wait()
    load_wo.wait()
    forward(0)
    pair_info.wait_recv()
    pair_x.wait_recv()
    xb[1] = xf[1].astype(BF16)
    forward(1)

    for c in hist_copies:
        c.wait_recv()
    totals = jnp.sum(hist[...], axis=0)
    inverse = 1.0 / jnp.maximum(totals, 1.0)
    own_weight = jnp.sum(match * inverse[0:1, :], axis=1, keepdims=True)
    weight[0] = jnp.broadcast_to(own_weight, (32, 128))
    pair_w = send(weight.at[0], weight.at[1], pair)

    backward(0)
    pair_y.wait_recv()
    pair_w.wait_recv()
    backward(1)

    def put(value, start, stride, size):
        for cb in range(value.shape[1] // 128):
            grad_flat[pl.ds(start + cb, size, stride=stride), :] = value[:, cb * 128 : cb * 128 + 128]

    grad_flat = grad.reshape(7168, 128)

    def out_terms(k):
        for n in range(3):
            part = dot(h_two[:, 256 * k : 256 * k + 256], e_all[:, 512 * n : 512 * n + 512], TN)
            put(part, 1024 + 3072 * k + 4 * n, 12, 256)

    @pl.when(r == 0)
    def _():
        for s in range(2):
            rows = slice(256 * s, 256 * s + 256)
            up = dot(b_two[rows, :], w_mid[...], NT)
            b_one[rows, :] = (slope_one[rows, :] * up).astype(BF16)
        for k in range(4):
            part = dot(xs[:, 256 * k : 256 * k + 256], b_one[...], TN)
            put(part[:128], 8 * k, 32, 128)
            put(part[128:], 8 * k + 4, 32, 128)

    @pl.when(r == 1)
    def _():
        put(dot(h_one[:, 256:512], b_two[...], TN), 0, 4, 256)
        out_terms(0)

    gx5 = grad.reshape(16, 4, 2, 56, 128)
    gy6 = grad.reshape(8, 2, 4, 2, 56, 128)
    gz = grad.reshape(8, 16, 56, 128)
    copies_z = []

    up_x, low_x, up_y, low_y = lax.rem(x + 1, 4), lax.rem(x + 3, 4), lax.rem(y + 1, 4), lax.rem(y + 3, 4)

    def for_x(to, part, rows):
        return gx5.at[8 * part : 8 * part + 8, to, :, rows, :]

    def for_y(to, part, rows):
        return gy6.at[4 * part : 4 * part + 4, to // 2, :, to % 2, rows, :]

    def far_part(part, at, size, far_x, far_y):
        rx_rows, ry_rows = slice(at, at + size), slice(24 + at, 24 + at + size)
        two_x, two_y = lax.rem(x + 2, 4), lax.rem(y + 2, 4)
        way = 1 + 2 * part
        return (
            send(for_x(two_x, part, rx_rows), far_x.at[part], along_x(way)),
            send(for_y(two_y, part, ry_rows), far_y.at[part], along_y(way)),
        )

    def far_phase(at, size, far_x, far_y):
        parts = [far_part(part, at, size, far_x, far_y) for part in range(2)]
        return [c[0] for c in parts], [c[1] for c in parts]

    def near_phase(at, size, from_x, from_y):
        rx_rows, ry_rows = slice(at, at + size), slice(24 + at, 24 + at + size)
        return (
            [
                send(for_x(up_x, 1, rx_rows), from_x.at[0, 1], along_x(1)),
                send(for_x(low_x, 0, rx_rows), from_x.at[1, 0], along_x(3)),
            ],
            [
                send(for_y(up_y, 1, ry_rows), from_y.at[0, 1], along_y(1)),
                send(for_y(low_y, 0, ry_rows), from_y.at[1, 0], along_y(3)),
            ],
        )

    def merge(at, size, far, near, far_x, far_y, from_x, from_y):
        rx_rows, ry_rows = slice(at, at + size), slice(24 + at, 24 + at + size)
        for part, to, way in ((0, up_x, 1), (1, low_x, 3)):
            far[0][part].wait_recv()
            for k in range(8):
                gx5[8 * part + k, to, :, rx_rows, :] = gx5[8 * part + k, to, :, rx_rows, :] + far_x[part, k]
            near[0].append(send(for_x(to, part, rx_rows), from_x.at[part, part], along_x(way)))
        for part, to, way in ((0, up_y, 1), (1, low_y, 3)):
            far[1][part].wait_recv()
            for k in range(4):
                there = (4 * part + k, to // 2, slice(None), to % 2, ry_rows, slice(None))
                gy6[there] = gy6[there] + far_y[part, k]
            near[1].append(send(for_y(to, part, ry_rows), from_y.at[part, part], along_y(way)))

    early = far_part(0, 0, 16, fx, fy)
    @pl.when(r == 0)
    def _():
        for k in range(2):
            part = dot(xs[:, 1024 + 256 * k : 1280 + 256 * k], b_one[...], TN)
            for m in range(4):
                put(part[64 * m : 64 * m + 64], 4096 + 4 * (4 * k + m), 32, 64)
        put(dot(h_one[:, 0:256], b_two[...], TN), 6144, 4, 256)

    @pl.when(r == 1)
    def _():
        out_terms(1)

    late = far_part(1, 0, 16, fx, fy)
    big_far = [early[0], late[0]], [early[1], late[1]]
    big_near = near_phase(0, 16, rx, ry)
    small_far = far_phase(16, 8, fxs, fys)
    for d in (4, 3, 5, 2, 6, 1, 7):
        copies_z.append(send(gz.at[lax.rem(z + d, 8), :, 48:56, :], rz.at[d - 1], along_z(d)))
    merge(0, 16, big_far, big_near, fx, fy, rx, ry)
    small_near = near_phase(16, 8, rxs, rys)

    for g in range(6):
        block_order(g, dot(perm[...], w_out[:, 256 * g : 256 * g + 256], NT), w_last)
    closure(xb[0])
    merge(16, 8, small_far, small_near, fxs, fys, rxs, rys)
    halo_finish(vp, 0, halo_one)

    def finish_one(c, bx, by, mid, rate):
        here = pl.ds(pl.multiple_of(by * 8 + 8, 8), 8)
        sp[c, pl.ds(bx * 8 + 1, 8), here, :] = mid + TIME_STEP * rate

    section(vp, finish_one)
    halo_two = halo_start(sp, 1)
    turn(take_from(sp))

    def write_second(at, tile):
        xb[1, :, at : at + 128] = tile.astype(BF16)

    rows_of(write_second)
    closure(xb[1])
    def second_phase(at, size, to_x, to_y, from_x, from_y, sum_x, sum_y, next_x, next_y):
        out_x, out_y = [], []
        for c in to_x:
            c.wait_recv()
        for k in range(16):
            sum_x[k] = gx5[k, x, :, at : at + size, :] + (from_x[0, k // 8, k % 8] + from_x[1, k // 8, k % 8])
        view = sum_x.reshape(8, 2, 2, size, 128)
        for d in range(1, 4):
            k = lax.rem(y + d, 4)
            out_x.append(send(view.at[:, k // 2, k % 2], next_x.at[d - 1], along_y(d)))
        for c in to_y:
            c.wait_recv()
        here = slice(24 + at, 24 + at + size)
        for k in range(8):
            sum_y[k] = gy6[k, yh, :, yl, here, :] + (from_y[0, k // 4, k % 4] + from_y[1, k // 4, k % 4])
        for d in range(1, 4):
            out_y.append(send(sum_y.at[:, lax.rem(x + d, 4)], next_y.at[d - 1], along_x(d)))
        return out_x, out_y

    def third_phase(size, out_x, out_y, sum_x, sum_y, next_x, next_y, both, arrived):
        view = sum_x.reshape(8, 2, 2, size, 128)
        for c in out_x:
            c.wait_recv()
        for k in range(8):
            both[k, 0:size, :] = view[k, yh, yl] + (next_x[0, k] + next_x[1, k] + next_x[2, k])
        for c in out_y:
            c.wait_recv()
        for k in range(8):
            both[k, size : 2 * size, :] = sum_y[k, x] + (next_y[0, k] + next_y[1, k] + next_y[2, k])
        return [send(both.at[lax.rem(z + d, 8)], arrived.at[d - 1], along_z(d)) for d in (4, 3, 5, 2, 6, 1, 7)]

    big_out_x, big_out_y = second_phase(0, 16, big_near[0], big_near[1], rx, ry, sx, sy, rx2, ry2)
    for c in copies_z:
        c.wait_recv()
    total = gz[z, :, 48:56, :]
    for d in range(7):
        total = total + rz[d]
    sz[...] = total.reshape(2, 4, 2, 8, 128)
    next_z = []
    for d in range(1, 4):
        next_z.append(send(sz.at[:, lax.rem(x + d, 4)], rz2.at[d - 1], along_x(d)))
    small_out_x, small_out_y = second_phase(16, 8, small_near[0], small_near[1], rxs, rys, sxs, syt, rx2s, ry2s)

    last_big = third_phase(16, big_out_x, big_out_y, sx, sy, rx2, ry2, sxy, rxy3)

    halo_finish(sp, 1, halo_two)

    def finish_two(c, bx, by, mid, rate):
        here = pl.ds(pl.multiple_of(by * 8 + 8, 8), 8)
        start = vp[c, pl.ds(bx * 8 + 1, 8), here, :]
        vnext[c, pl.ds(bx * 8, 8), pl.ds(pl.multiple_of(by * 8, 8), 8), :] = 0.75 * start + 0.25 * (
            mid + TIME_STEP * rate
        )

    section(sp, finish_two)

    for c in next_z:
        c.wait_recv()
    sz2[...] = sz[:, x] + (rz2[0] + rz2[1] + rz2[2])
    last_z = []
    for d in range(1, 4):
        k = lax.rem(y + d, 4)
        last_z.append(send(sz2.at[k // 2, k % 2], rz3.at[d - 1], along_y(d)))
    last_small = third_phase(8, small_out_x, small_out_y, sxs, syt, rx2s, ry2s, sxys, rxy3s)
    for c in last_big + last_z + last_small:
        c.wait_recv()
    front = sxy[z]
    tail = sxys[z]
    for d in range(7):
        front = front + rxy3[d]
        tail = tail + rxy3s[d]
    back = sz2[yh, yl] + (rz3[0] + rz3[1] + rz3[2])
    g = jnp.concatenate([front[:16], tail[:8], front[16:], tail[8:], back], axis=0)
    moment = BETA_ONE * mom1[...] + (1.0 - BETA_ONE) * g
    second = BETA_TWO * mom2[...] + (1.0 - BETA_TWO) * g * g
    corrected = moment / (1.0 - BETA_ONE**ADAM_STEP)
    direction[...] = corrected / (jnp.sqrt(second / (1.0 - BETA_TWO**ADAM_STEP)) + EPSILON)

    for c in (
        hist_copies + [pair_info, pair_y, pair_x, pair_w] + halo_one + halo_two
        + big_far[0] + big_far[1] + big_near[0] + big_near[1] + small_far[0] + small_far[1]
        + small_near[0] + small_near[1] + copies_z + big_out_x + big_out_y + small_out_x + small_out_y
        + next_z + last_big + last_small + last_z
    ):
        c.wait_send()


def local(velocity, target_field, w_in, w_mid, w_out, moment_one, moment_two, picks, owners, counts):
    any_space = pl.BlockSpec(memory_space=pl.ANY)
    vmem = pl.BlockSpec(memory_space=pltpu.VMEM)
    V = pltpu.VMEM
    next_velocity, direction = pl.pallas_call(
        kernel,
        out_shape=(
            pltpu.VMEM(velocity.shape, F32),
            pltpu.VMEM((56, 128), F32),
        ),
        in_specs=[any_space] * 5 + [vmem] * 5,
        out_specs=(vmem, vmem),
        scratch_shapes=[
            V((3, 26, 40, 128), F32),
            V((3, 26, 40, 128), F32),
            V((3, 24, 24, 128), F32),
            V((1536, 512), BF16),
            V((512, 512), BF16),
            V((512, 1536), BF16),
            V((1536, 512), BF16),
            V((1536, 512), BF16),
            V((256, 256), BF16),
            V((1152, 128), F32),
            V((1152, 128), F32),
            V((2, ROWS, WIDE), F32),
            V((2, ROWS, WIDE), BF16),
            V((2, ROWS, WIDE), F32),
            V((2, 32, 128), F32),
            V((2, 32, 128), F32),
            V((8, 128), F32),
            V((16, 8, 128), F32),
            V((2, 2, 3, 24, 128), F32),
            V((2, 2, 3, 24, 128), F32),
            V((512, WIDE), BF16),
            V((512, 512), F32),
            V((512, 512), F32),
            V((512, 512), BF16),
            V((512, 512), BF16),
            V((512, WIDE), BF16),
            V((512, 512), BF16),
            V((512, 512), BF16),
            V((7168, 128), F32),
            V((2, 2, 8, 2, 16, 128), F32),
            V((2, 2, 4, 4, 16, 128), F32),
            V((7, 16, 8, 128), F32),
            V((16, 2, 16, 128), F32),
            V((8, 4, 16, 128), F32),
            V((2, 4, 2, 8, 128), F32),
            V((3, 8, 16, 128), F32),
            V((3, 8, 16, 128), F32),
            V((3, 2, 2, 8, 128), F32),
            V((8, 32, 128), F32),
            V((2, 2, 8, 128), F32),
            V((7, 32, 128), F32),
            V((3, 8, 128), F32),
            V((2, 2, 8, 2, 8, 128), F32),
            V((2, 2, 4, 4, 8, 128), F32),
            V((16, 2, 8, 128), F32),
            V((8, 4, 8, 128), F32),
            V((3, 8, 8, 128), F32),
            V((3, 8, 8, 128), F32),
            V((8, 16, 128), F32),
            V((7, 16, 128), F32),
            V((2, 8, 2, 16, 128), F32),
            V((2, 4, 4, 16, 128), F32),
            V((2, 8, 2, 8, 128), F32),
            V((2, 4, 4, 8, 128), F32),
            pltpu.SemaphoreType.DMA((5,)),
            pltpu.SemaphoreType.DMA((90,)),
            pltpu.SemaphoreType.DMA((90,)),
        ],
        compiler_params=pltpu.CompilerParams(
            collective_id=0, has_side_effects=True, vmem_limit_bytes=60 * 2**20
        ),
    )(
        velocity, target_field, w_in, w_mid, w_out,
        moment_one.reshape(56, 128), moment_two.reshape(56, 128),
        picks.reshape(1, 32), owners.reshape(1, 32), counts,
    )
    return next_velocity, direction.reshape(7168)


def solution(mesh):
    return jax.shard_map(
        local,
        mesh=mesh,
        in_specs=(
            P(None, "gx", ("role", "gy"), None),
            P(None, "gx", ("role", "gy"), None),
            P(),
            P(),
            P(),
            P(("role", "gx", "gy")),
            P(("role", "gx", "gy")),
            P(("role", "gx", "gy")),
            P(("role", "gx", "gy")),
            P(("role", "gy"), "gx"),
        ),
        out_specs=(P(None, "gx", ("role", "gy"), None), P(("role", "gx", "gy"))),
        check_vma=False,
    )
```

```python
import math

import jax
import jax.numpy as jnp
from jax import lax
from jax.experimental import pallas as pl
from jax.experimental.pallas import tpu as pltpu
from jax.sharding import PartitionSpec as P

ADAM_STEP = 10
TIME_STEP = 0.2
VISCOSITY = 0.05
BETA_ONE = 0.9
BETA_TWO = 0.999
EPSILON = 1e-08
MESH = pl.DeviceIdType.MESH
F32 = jnp.float32
BF16 = jnp.bfloat16
NN = (((1,), (0,)), ((), ()))
NT = (((1,), (1,)), ((), ()))
TN = (((0,), (0,)), ((), ()))
GELU_K = math.sqrt(2.0 / math.pi)
GELU_C = 0.044715
ROWS = 144
WIDE = 1536


def dot(a, b, dims=NN):
    return lax.dot_general(a, b, dims, preferred_element_type=F32)


def gelu(a):
    t = jnp.tanh(GELU_K * (a + GELU_C * (a * a * a)))
    return a * (0.5 * (1.0 + t))


def gelu_and_slope(a):
    a2 = a * a
    t = jnp.tanh(GELU_K * (a + GELU_C * (a2 * a)))
    cdf = 0.5 * (1.0 + t)
    slope = cdf + (0.5 * GELU_K) * a * (1.0 - t * t) * (1.0 + (3.0 * GELU_C) * a2)
    return a * cdf, slope


def place(r, z, yh, x, yl):
    return {"role": r, "gx": z * 2 + yh, "gy": x * 2 + yl}


def kernel(
    vel_hbm, tgt_hbm, win_hbm, wmid_hbm, wout_hbm, mom1, mom2, picks, owners, counts,
    vnext, direction,
    vp, sp, tgt, w_in, w_mid, w_out, w_first, w_last, perm,
    t_zero, t_one, xf, xb, yf, info, weight, hist_out, hist, ysend, yrecv,
    xs, slope_one, slope_two, h_one, h_two, e_all, b_two, b_one,
    grad, rx, ry, rz, sx, sy, sz, rx2, ry2, rz2, sxy, sz2, rxy3, rz3,
    rxs, rys, sxs, syt, rx2s, ry2s, sxys, rxy3s, fx, fy, fxs, fys, miss,
    load_sem, send_sem, recv_sem,
):
    r = lax.axis_index("role")
    i = lax.axis_index("gx")
    j = lax.axis_index("gy")
    z, yh, x, yl = i // 2, i % 2, j // 2, j % 2
    y = yh * 2 + yl
    q = r * 8 + j

    def at_q(k):
        k = lax.rem(k + 16, 16)
        return {"role": k // 8, "gx": i, "gy": k % 8}

    def at_i(k):
        return {"role": r, "gx": lax.rem(k + 16, 16), "gy": j}

    def along_x(d):
        return place(r, z, yh, lax.rem(x + d, 4), yl)

    def along_y(d):
        k = lax.rem(y + d, 4)
        return place(r, z, k // 2, x, k % 2)

    def along_z(d):
        return place(r, lax.rem(z + d, 8), yh, x, yl)

    pair = {"role": 1 - r, "gx": i, "gy": j}

    loads = []

    def load(src, dst):
        c = pltpu.make_async_copy(src, dst, load_sem.at[len(loads)])
        c.start()
        loads.append(c)
        return c

    load_v = load(vel_hbm, vp.at[:, 1:25, 8:32, :])
    load_t = load(tgt_hbm, tgt)
    load_wi = load(win_hbm, w_in)
    load_wo = load(wout_hbm, w_out)
    load_wm = load(wmid_hbm, w_mid)

    barrier = pltpu.get_barrier_semaphore()
    other = at_q(q + 2 * yl - 1)
    for d in (8, 7, 9, 6, 10, 5, 11, 4, 12, 3, 13, 2, 14, 1, 15):
        pl.semaphore_signal(barrier, inc=1, device_id=at_i(i + d), device_id_type=MESH)
    for d in range(1, 4):
        pl.semaphore_signal(barrier, inc=1, device_id=along_x(d), device_id_type=MESH)
    for who in (place(r, z, yh, x, 1 - yl), place(r, z, 1 - yh, x, 1 - yl), pair, other):
        pl.semaphore_signal(barrier, inc=1, device_id=who, device_id_type=MESH)

    def column(row):
        a = lax.broadcasted_iota(jnp.int32, (32, 32), 0)
        b = lax.broadcasted_iota(jnp.int32, (32, 32), 1)
        picked = jnp.where(a == b, jnp.broadcast_to(row, (32, 32)), 0.0)
        return jnp.broadcast_to(jnp.sum(picked, axis=1, keepdims=True), (32, 128))

    o = picks[...]
    one, nil = jnp.ones_like(o), jnp.zeros_like(o)
    over30 = jnp.where(o >= 30, one, nil)
    over15 = jnp.where(o >= 15, one, nil) + over30 + jnp.where(o >= 45, one, nil)
    first_block = (over30 * 3 + (over15 - 2 * over30)) * 16 + (o - 15 * over15)
    info[0] = column(first_block.astype(F32))
    owner = column(owners[...].astype(F32))
    slot = lax.broadcasted_iota(jnp.int32, (32, 128), 0)
    lane = lax.broadcasted_iota(jnp.int32, (32, 128), 1).astype(F32)
    alive = slot < jnp.broadcast_to(counts[...], (32, 128))
    match = jnp.where(alive, jnp.where(lane == owner, 1.0, 0.0), 0.0)
    hist_out[...] = jnp.broadcast_to(jnp.sum(match, axis=0, keepdims=True), (8, 128))
    hist[pl.ds(i, 1)] = hist_out[...].reshape(1, 8, 128)

    count = [0]

    def send(src, dst, who):
        k = count[0]
        count[0] += 1
        c = pltpu.make_async_remote_copy(
            src_ref=src, dst_ref=dst, send_sem=send_sem.at[k], recv_sem=recv_sem.at[k],
            device_id=who, device_id_type=MESH,
        )
        c.start()
        return c

    def halo_start(field, slot):
        flat = field.reshape(3 * 26 * 40, 128)
        for c in range(3):
            ysend[slot, 0, c] = flat[pl.ds((c * 26 + 1) * 40 + 8, 24, stride=40), :]
            ysend[slot, 1, c] = flat[pl.ds((c * 26 + 1) * 40 + 31, 24, stride=40), :]
        return [
            send(field.at[:, 1, 8:32, :], field.at[:, 25, 8:32, :], at_i(i - 1)),
            send(field.at[:, 24, 8:32, :], field.at[:, 0, 8:32, :], at_i(i + 1)),
            send(ysend.at[slot, 0], yrecv.at[slot, 1], at_q(q - 1)),
            send(ysend.at[slot, 1], yrecv.at[slot, 0], at_q(q + 1)),
        ]

    def halo_finish(field, slot, copies):
        for c in copies:
            c.wait_recv()
        flat = field.reshape(3 * 26 * 40, 128)
        for c in range(3):
            flat[pl.ds((c * 26 + 1) * 40 + 7, 24, stride=40), :] = yrecv[slot, 0, c]
            flat[pl.ds((c * 26 + 1) * 40 + 32, 24, stride=40), :] = yrecv[slot, 1, c]

    def turn(take):
        def body(k, carry):
            d = take(k // 3, k % 3).reshape(192, 128)
            rows = pl.ds(pl.multiple_of(k * 128, 128), 128)
            t_zero[rows, :] = d[:128].T
            t_one[rows, 0:64] = d[128:].T
            return carry

        lax.fori_loop(0, 9, body, 0)

    def take_from(field):
        def take(bx, by):
            return field[:, pl.ds(bx * 8 + 1, 8), pl.ds(pl.multiple_of(by * 8 + 8, 8), 8), :]

        return take

    half = lax.broadcasted_iota(jnp.int32, (ROWS, 128), 1)

    def rows_of(write):
        for oz in range(8):
            write(oz * 128, t_zero[pl.ds(oz, ROWS, stride=8), :])
        for k in range(4):
            a = t_one[pl.ds(2 * k, ROWS, stride=8), :]
            b = t_one[pl.ds(2 * k + 1, ROWS, stride=8), :]
            write(1024 + k * 128, jnp.where(half < 64, a, pltpu.roll(b, 64, 1)))

    pr = lax.broadcasted_iota(jnp.int32, (256, 256), 0)
    pc = lax.broadcasted_iota(jnp.int32, (256, 256), 1)
    perm[...] = jnp.where(pc == (pr & 31) * 8 + (pr >> 5), 1.0, 0.0).astype(BF16)

    pl.semaphore_wait(barrier, 22)
    hist_copies = [send(hist_out, hist.at[i], at_i(i + d)) for d in (8, 7, 9, 6, 10, 5, 11, 4, 12, 3, 13, 2, 14, 1, 15)]
    pair_info = send(info.at[0], info.at[1], pair)

    load_v.wait()
    turn(take_from(vp))

    def write_x(at, tile):
        xf[0, :, at : at + 128] = tile
        xb[0, :, at : at + 128] = tile.astype(BF16)

    rows_of(write_x)

    pair_x = send(xf.at[0], xf.at[1], pair)
    halo_one = halo_start(vp, 0)

    load_t.wait()

    def take_target(bx, by):
        return tgt[:, pl.ds(bx * 8, 8), pl.ds(pl.multiple_of(by * 8, 8), 8), :]

    turn(take_target)
    for g in range(6):
        tiles = []
        src, base = (t_zero, g) if g < 4 else (t_one, g - 4)
        for quad in range(2):
            tile = None
            for m in range(4):
                part = src[pl.ds(4 * quad + m, ROWS, stride=8), :]
                shift = (32 * (m - base)) % 128
                if shift:
                    part = pltpu.roll(part, shift, 1)
                tile = part if tile is None else jnp.where(half >= 32 * m, part, tile)
            tiles.append(tile.astype(BF16))
        yf[0, :, 256 * g : 256 * g + 256] = dot(jnp.concatenate(tiles, axis=1), perm[...])
    pair_y = send(yf.at[0], yf.at[1], pair)

    def block_order(g, value, dst):
        for oz in range(8):
            at = oz * 128 + 32 * g if g < 4 else 1024 + oz * 64 + 32 * (g - 4)
            dst[at : at + 32, :] = value[32 * oz : 32 * oz + 32].astype(BF16)

    load_wi.wait()
    for g in range(6):
        block_order(g, dot(perm[...], w_in[256 * g : 256 * g + 256, :]), w_first)

    def choose(s):
        start = info[s]
        start = jnp.concatenate([start, start], axis=1)[:, :ROWS]
        block = lax.broadcasted_iota(jnp.int32, (32, ROWS), 1).astype(F32)
        return jnp.concatenate(
            [
                jnp.where(block == start + float(k // 4 * 48 + k // 2 % 2 * 16 + k % 2), 1.0, 0.0)
                for k in range(8)
            ],
            axis=0,
        ).astype(BF16)

    def forward(s):
        rows = slice(256 * s, 256 * s + 256)
        chosen = choose(s)
        for n in range(3):
            cols = slice(512 * n, 512 * n + 512)
            xs[rows, cols] = dot(chosen, xb[s, :, cols]).astype(BF16)
        a, slope = gelu_and_slope(dot(xs[rows, :], w_first[...]))
        slope_one[rows, :] = slope
        h1 = a.astype(BF16)
        h_one[rows, :] = h1
        a, slope = gelu_and_slope(dot(h1, w_mid[...]))
        slope_two[rows, :] = slope
        h_two[rows, :] = a.astype(BF16)

    def compare(s):
        rows = slice(256 * s, 256 * s + 256)
        chosen = choose(s)
        for n in range(3):
            cols = slice(512 * n, 512 * n + 512)
            target = dot(chosen, yf[s, :, cols].astype(BF16))
            miss[rows, cols] = dot(h_two[rows, :], w_out[:, cols]) - target

    def backward(s):
        rows = slice(256 * s, 256 * s + 256)
        w8 = 2.0 * jnp.concatenate([weight[s]] * 8, axis=0)
        w8 = jnp.concatenate([w8] * 4, axis=1)
        up = None
        for n in range(3):
            cols = slice(512 * n, 512 * n + 512)
            e = (w8 * miss[rows, cols]).astype(BF16)
            e_all[rows, cols] = e
            part = dot(e, w_out[:, cols], NT)
            up = part if up is None else up + part
        b_two[rows, :] = (slope_two[rows, :] * up).astype(BF16)

    def closure(rows):
        q1 = gelu(dot(rows, w_first[...])).astype(BF16)
        q2 = gelu(dot(q1, w_mid[...])).astype(BF16)
        for n in range(2):
            out = dot(q2, w_last[512 * n : 512 * n + 512, :], NT)
            for m in range(4):
                t_zero[pl.ds(4 * n + m, ROWS, stride=8), :] = out[:, 128 * m : 128 * m + 128]
        out = dot(q2, w_last[1024:1536, :], NT)
        for m in range(4):
            tile = out[:, 128 * m : 128 * m + 128]
            t_one[pl.ds(2 * m, ROWS, stride=8), :] = tile
            t_one[pl.ds(2 * m + 1, ROWS, stride=8), :] = pltpu.roll(tile, 64, 1)

    def section(field, finish):
        def body(k, carry):
            bx, by = k // 3, k % 3
            rows = pl.ds(pl.multiple_of(k * 128, 128), 128)
            closed = [None, None, None]
            front = t_zero[rows, :].T
            closed[0] = front[:64].reshape(8, 8, 128)
            closed[1] = front[64:].reshape(8, 8, 128)
            closed[2] = t_one[rows, :].T[:64].reshape(8, 8, 128)
            here = pl.ds(pl.multiple_of(by * 8 + 8, 8), 8)
            around = pl.ds(pl.multiple_of(by * 8, 8), 24)
            center = [field[c, pl.ds(bx * 8 + 1, 8), here, :] for c in range(3)]
            for c in range(3):
                mid = center[c]
                first_up = field[c, pl.ds(bx * 8 + 2, 8), here, :]
                first_down = field[c, pl.ds(bx * 8, 8), here, :]
                window = field[c, pl.ds(bx * 8 + 1, 8), around, :]
                second_up = window[:, 9:17, :]
                second_down = window[:, 7:15, :]
                third_up = pltpu.roll(mid, 127, 2)
                third_down = pltpu.roll(mid, 1, 2)
                advect = (
                    center[0] * ((first_up - first_down) * 0.5)
                    + center[1] * ((second_up - second_down) * 0.5)
                    + center[2] * ((third_up - third_down) * 0.5)
                )
                spread = (
                    first_up + first_down + (second_up + second_down) + (third_up + third_down) - 6.0 * mid
                )
                finish(c, bx, by, mid, VISCOSITY * spread - advect + closed[c])
            return carry

        lax.fori_loop(0, 9, body, 0)

    load_wm.wait()
    load_wo.wait()
    forward(0)
    compare(0)
    pair_info.wait_recv()
    pair_x.wait_recv()
    xb[1] = xf[1].astype(BF16)
    forward(1)

    for c in hist_copies:
        c.wait_recv()
    totals = jnp.sum(hist[...], axis=0)
    inverse = 1.0 / jnp.maximum(totals, 1.0)
    own_weight = jnp.sum(match * inverse[0:1, :], axis=1, keepdims=True)
    weight[0] = jnp.broadcast_to(own_weight, (32, 128))
    pair_w = send(weight.at[0], weight.at[1], pair)

    backward(0)
    pair_y.wait_recv()
    compare(1)
    pair_w.wait_recv()
    backward(1)

    def put(value, start, stride, size):
        for cb in range(value.shape[1] // 128):
            grad_flat[pl.ds(start + cb, size, stride=stride), :] = value[:, cb * 128 : cb * 128 + 128]

    grad_flat = grad.reshape(7168, 128)

    def out_terms(k):
        for n in range(3):
            part = dot(h_two[:, 256 * k : 256 * k + 256], e_all[:, 512 * n : 512 * n + 512], TN)
            put(part, 1024 + 3072 * k + 4 * n, 12, 256)

    @pl.when(r == 0)
    def _():
        for s in range(2):
            rows = slice(256 * s, 256 * s + 256)
            up = dot(b_two[rows, :], w_mid[...], NT)
            b_one[rows, :] = (slope_one[rows, :] * up).astype(BF16)
        for k in range(4):
            part = dot(xs[:, 256 * k : 256 * k + 256], b_one[...], TN)
            put(part[:128], 8 * k, 32, 128)
            put(part[128:], 8 * k + 4, 32, 128)

    @pl.when(r == 1)
    def _():
        put(dot(h_one[:, 256:512], b_two[...], TN), 0, 4, 256)
        out_terms(0)

    gx5 = grad.reshape(16, 4, 2, 56, 128)
    gy6 = grad.reshape(8, 2, 4, 2, 56, 128)
    gz = grad.reshape(8, 16, 56, 128)
    copies_z = []

    up_x, low_x, up_y, low_y = lax.rem(x + 1, 4), lax.rem(x + 3, 4), lax.rem(y + 1, 4), lax.rem(y + 3, 4)

    def for_x(to, part, rows):
        return gx5.at[8 * part : 8 * part + 8, to, :, rows, :]

    def for_y(to, part, rows):
        return gy6.at[4 * part : 4 * part + 4, to // 2, :, to % 2, rows, :]

    def far_part(part, at, size, far_x, far_y):
        rx_rows, ry_rows = slice(at, at + size), slice(24 + at, 24 + at + size)
        two_x, two_y = lax.rem(x + 2, 4), lax.rem(y + 2, 4)
        way = 1 + 2 * part
        return (
            send(for_x(two_x, part, rx_rows), far_x.at[part], along_x(way)),
            send(for_y(two_y, part, ry_rows), far_y.at[part], along_y(way)),
        )

    def far_phase(at, size, far_x, far_y):
        parts = [far_part(part, at, size, far_x, far_y) for part in range(2)]
        return [c[0] for c in parts], [c[1] for c in parts]

    def near_phase(at, size, from_x, from_y):
        rx_rows, ry_rows = slice(at, at + size), slice(24 + at, 24 + at + size)
        return (
            [
                send(for_x(up_x, 1, rx_rows), from_x.at[0, 1], along_x(1)),
                send(for_x(low_x, 0, rx_rows), from_x.at[1, 0], along_x(3)),
            ],
            [
                send(for_y(up_y, 1, ry_rows), from_y.at[0, 1], along_y(1)),
                send(for_y(low_y, 0, ry_rows), from_y.at[1, 0], along_y(3)),
            ],
        )

    def merge(at, size, far, near, far_x, far_y, from_x, from_y):
        rx_rows, ry_rows = slice(at, at + size), slice(24 + at, 24 + at + size)
        for part, to, way in ((0, up_x, 1), (1, low_x, 3)):
            far[0][part].wait_recv()
            for k in range(8):
                gx5[8 * part + k, to, :, rx_rows, :] = gx5[8 * part + k, to, :, rx_rows, :] + far_x[part, k]
            near[0].append(send(for_x(to, part, rx_rows), from_x.at[part, part], along_x(way)))
        for part, to, way in ((0, up_y, 1), (1, low_y, 3)):
            far[1][part].wait_recv()
            for k in range(4):
                there = (4 * part + k, to // 2, slice(None), to % 2, ry_rows, slice(None))
                gy6[there] = gy6[there] + far_y[part, k]
            near[1].append(send(for_y(to, part, ry_rows), from_y.at[part, part], along_y(way)))

    early = far_part(0, 0, 16, fx, fy)
    @pl.when(r == 0)
    def _():
        for k in range(2):
            part = dot(xs[:, 1024 + 256 * k : 1280 + 256 * k], b_one[...], TN)
            for m in range(4):
                put(part[64 * m : 64 * m + 64], 4096 + 4 * (4 * k + m), 32, 64)
        put(dot(h_one[:, 0:256], b_two[...], TN), 6144, 4, 256)

    @pl.when(r == 1)
    def _():
        out_terms(1)

    late = far_part(1, 0, 16, fx, fy)
    big_far = [early[0], late[0]], [early[1], late[1]]
    big_near = near_phase(0, 16, rx, ry)
    small_far = far_phase(16, 8, fxs, fys)
    for d in (4, 3, 5, 2, 6, 1, 7):
        copies_z.append(send(gz.at[lax.rem(z + d, 8), :, 48:56, :], rz.at[d - 1], along_z(d)))
    merge(0, 16, big_far, big_near, fx, fy, rx, ry)
    small_near = near_phase(16, 8, rxs, rys)

    for g in range(6):
        block_order(g, dot(perm[...], w_out[:, 256 * g : 256 * g + 256], NT), w_last)
    closure(xb[0])
    merge(16, 8, small_far, small_near, fxs, fys, rxs, rys)
    halo_finish(vp, 0, halo_one)

    def finish_one(c, bx, by, mid, rate):
        here = pl.ds(pl.multiple_of(by * 8 + 8, 8), 8)
        sp[c, pl.ds(bx * 8 + 1, 8), here, :] = mid + TIME_STEP * rate

    section(vp, finish_one)
    halo_two = halo_start(sp, 1)
    turn(take_from(sp))

    def write_second(at, tile):
        xb[1, :, at : at + 128] = tile.astype(BF16)

    rows_of(write_second)
    closure(xb[1])
    def second_phase(at, size, to_x, to_y, from_x, from_y, sum_x, sum_y, next_x, next_y):
        out_x, out_y = [], []
        for c in to_x:
            c.wait_recv()
        for k in range(16):
            sum_x[k] = gx5[k, x, :, at : at + size, :] + (from_x[0, k // 8, k % 8] + from_x[1, k // 8, k % 8])
        view = sum_x.reshape(8, 2, 2, size, 128)
        for d in range(1, 4):
            k = lax.rem(y + d, 4)
            out_x.append(send(view.at[:, k // 2, k % 2], next_x.at[d - 1], along_y(d)))
        for c in to_y:
            c.wait_recv()
        here = slice(24 + at, 24 + at + size)
        for k in range(8):
            sum_y[k] = gy6[k, yh, :, yl, here, :] + (from_y[0, k // 4, k % 4] + from_y[1, k // 4, k % 4])
        for d in range(1, 4):
            out_y.append(send(sum_y.at[:, lax.rem(x + d, 4)], next_y.at[d - 1], along_x(d)))
        return out_x, out_y

    def third_phase(size, out_x, out_y, sum_x, sum_y, next_x, next_y, both, arrived):
        view = sum_x.reshape(8, 2, 2, size, 128)
        for c in out_x:
            c.wait_recv()
        for k in range(8):
            both[k, 0:size, :] = view[k, yh, yl] + (next_x[0, k] + next_x[1, k] + next_x[2, k])
        for c in out_y:
            c.wait_recv()
        for k in range(8):
            both[k, size : 2 * size, :] = sum_y[k, x] + (next_y[0, k] + next_y[1, k] + next_y[2, k])
        return [send(both.at[lax.rem(z + d, 8)], arrived.at[d - 1], along_z(d)) for d in (4, 3, 5, 2, 6, 1, 7)]

    big_out_x, big_out_y = second_phase(0, 16, big_near[0], big_near[1], rx, ry, sx, sy, rx2, ry2)
    for c in copies_z:
        c.wait_recv()
    total = gz[z, :, 48:56, :]
    for d in range(7):
        total = total + rz[d]
    sz[...] = total.reshape(2, 4, 2, 8, 128)
    next_z = []
    for d in range(1, 4):
        next_z.append(send(sz.at[:, lax.rem(x + d, 4)], rz2.at[d - 1], along_x(d)))
    small_out_x, small_out_y = second_phase(16, 8, small_near[0], small_near[1], rxs, rys, sxs, syt, rx2s, ry2s)

    last_big = third_phase(16, big_out_x, big_out_y, sx, sy, rx2, ry2, sxy, rxy3)

    halo_finish(sp, 1, halo_two)

    def finish_two(c, bx, by, mid, rate):
        here = pl.ds(pl.multiple_of(by * 8 + 8, 8), 8)
        start = vp[c, pl.ds(bx * 8 + 1, 8), here, :]
        vnext[c, pl.ds(bx * 8, 8), pl.ds(pl.multiple_of(by * 8, 8), 8), :] = 0.75 * start + 0.25 * (
            mid + TIME_STEP * rate
        )

    section(sp, finish_two)

    for c in next_z:
        c.wait_recv()
    sz2[...] = sz[:, x] + (rz2[0] + rz2[1] + rz2[2])
    last_z = []
    for d in range(1, 4):
        k = lax.rem(y + d, 4)
        last_z.append(send(sz2.at[k // 2, k % 2], rz3.at[d - 1], along_y(d)))
    last_small = third_phase(8, small_out_x, small_out_y, sxs, syt, rx2s, ry2s, sxys, rxy3s)
    for c in last_big + last_z + last_small:
        c.wait_recv()
    front = sxy[z]
    tail = sxys[z]
    for d in range(7):
        front = front + rxy3[d]
        tail = tail + rxy3s[d]
    back = sz2[yh, yl] + (rz3[0] + rz3[1] + rz3[2])
    g = jnp.concatenate([front[:16], tail[:8], front[16:], tail[8:], back], axis=0)
    moment = BETA_ONE * mom1[...] + (1.0 - BETA_ONE) * g
    second = BETA_TWO * mom2[...] + (1.0 - BETA_TWO) * g * g
    corrected = moment / (1.0 - BETA_ONE**ADAM_STEP)
    direction[...] = corrected / (jnp.sqrt(second / (1.0 - BETA_TWO**ADAM_STEP)) + EPSILON)

    for c in (
        hist_copies + [pair_info, pair_y, pair_x, pair_w] + halo_one + halo_two
        + big_far[0] + big_far[1] + big_near[0] + big_near[1] + small_far[0] + small_far[1]
        + small_near[0] + small_near[1] + copies_z + big_out_x + big_out_y + small_out_x + small_out_y
        + next_z + last_big + last_small + last_z
    ):
        c.wait_send()


def local(velocity, target_field, w_in, w_mid, w_out, moment_one, moment_two, picks, owners, counts):
    any_space = pl.BlockSpec(memory_space=pl.ANY)
    vmem = pl.BlockSpec(memory_space=pltpu.VMEM)
    V = pltpu.VMEM
    next_velocity, direction = pl.pallas_call(
        kernel,
        out_shape=(
            pltpu.VMEM(velocity.shape, F32),
            pltpu.VMEM((56, 128), F32),
        ),
        in_specs=[any_space] * 5 + [vmem] * 5,
        out_specs=(vmem, vmem),
        scratch_shapes=[
            V((3, 26, 40, 128), F32),
            V((3, 26, 40, 128), F32),
            V((3, 24, 24, 128), F32),
            V((1536, 512), BF16),
            V((512, 512), BF16),
            V((512, 1536), BF16),
            V((1536, 512), BF16),
            V((1536, 512), BF16),
            V((256, 256), BF16),
            V((1152, 128), F32),
            V((1152, 128), F32),
            V((2, ROWS, WIDE), F32),
            V((2, ROWS, WIDE), BF16),
            V((2, ROWS, WIDE), F32),
            V((2, 32, 128), F32),
            V((2, 32, 128), F32),
            V((8, 128), F32),
            V((16, 8, 128), F32),
            V((2, 2, 3, 24, 128), F32),
            V((2, 2, 3, 24, 128), F32),
            V((512, WIDE), BF16),
            V((512, 512), F32),
            V((512, 512), F32),
            V((512, 512), BF16),
            V((512, 512), BF16),
            V((512, WIDE), BF16),
            V((512, 512), BF16),
            V((512, 512), BF16),
            V((7168, 128), F32),
            V((2, 2, 8, 2, 16, 128), F32),
            V((2, 2, 4, 4, 16, 128), F32),
            V((7, 16, 8, 128), F32),
            V((16, 2, 16, 128), F32),
            V((8, 4, 16, 128), F32),
            V((2, 4, 2, 8, 128), F32),
            V((3, 8, 16, 128), F32),
            V((3, 8, 16, 128), F32),
            V((3, 2, 2, 8, 128), F32),
            V((8, 32, 128), F32),
            V((2, 2, 8, 128), F32),
            V((7, 32, 128), F32),
            V((3, 8, 128), F32),
            V((2, 2, 8, 2, 8, 128), F32),
            V((2, 2, 4, 4, 8, 128), F32),
            V((16, 2, 8, 128), F32),
            V((8, 4, 8, 128), F32),
            V((3, 8, 8, 128), F32),
            V((3, 8, 8, 128), F32),
            V((8, 16, 128), F32),
            V((7, 16, 128), F32),
            V((2, 8, 2, 16, 128), F32),
            V((2, 4, 4, 16, 128), F32),
            V((2, 8, 2, 8, 128), F32),
            V((2, 4, 4, 8, 128), F32),
            V((512, WIDE), F32),
            pltpu.SemaphoreType.DMA((5,)),
            pltpu.SemaphoreType.DMA((90,)),
            pltpu.SemaphoreType.DMA((90,)),
        ],
        compiler_params=pltpu.CompilerParams(
            collective_id=0, has_side_effects=True, vmem_limit_bytes=60 * 2**20
        ),
    )(
        velocity, target_field, w_in, w_mid, w_out,
        moment_one.reshape(56, 128), moment_two.reshape(56, 128),
        picks.reshape(1, 32), owners.reshape(1, 32), counts,
    )
    return next_velocity, direction.reshape(7168)


def solution(mesh):
    return jax.shard_map(
        local,
        mesh=mesh,
        in_specs=(
            P(None, "gx", ("role", "gy"), None),
            P(None, "gx", ("role", "gy"), None),
            P(),
            P(),
            P(),
            P(("role", "gx", "gy")),
            P(("role", "gx", "gy")),
            P(("role", "gx", "gy")),
            P(("role", "gx", "gy")),
            P(("role", "gy"), "gx"),
        ),
        out_specs=(P(None, "gx", ("role", "gy"), None), P(("role", "gx", "gy"))),
        check_vma=False,
    )
```
